32 devices in a mesh: space: 8 (over z, x), dp: 4 (over y, core).
Axes of the slice: x: 2, y: 2, z: 4, core: 2. Of those that a mesh axis runs over, the one named last changes fastest.
Arguments:
- features: bfloat16 [4, 4096, 128], P('dp', 'space'), may hold values from -6 to 6
- cotangent: bfloat16 [4, 4096, 128], P('dp', 'space'), may hold values from -6 to 6
- weight_one: bfloat16 [27, 128, 128], replicated, may hold values from -0.21875 to 0.21875
- weight_two: bfloat16 [27, 128, 128], replicated, may hold values from -0.21875 to 0.21875
- rules: int32 [4, 8, 2, 27, 256], P('dp', 'space'), may hold values from 0 to 1024, as said below
- halo_send: int32 [4, 8, 2, 2], P('dp', 'space'), may hold values from 0 to 3
- block_counts: int32 [4, 32], P('dp', 'space'), may hold values from 16 to 128
Outputs:
- grad_features: float32 [4, 4096, 128], P('dp', 'space')
- grad_one: float32 [27, 128, 128], replicated
- grad_two: float32 [27, 128, 128], replicated
The draws below stay inside these ranges and needn't reach their ends.
Inputs may be any that keep to these rules, and one draw needn't show every extreme that they name: `rules`: for each scene, slab and offset, the live slots come first and hold distinct targets and distinct sources; padding slots hold source 1024 and target 512; at least half of the slots are live, and offset 13 is full with each source equal to its target.
All inputs are finite; a program needn't handle non-finite values.
Results may differ from the reference program's by a relative error of at most 0.0032.
Values may be sent and summed in bfloat16 or wider, within the bound.
A program may use at most 64 MiB of HBM per device.

```python
import jax
import jax.numpy as jnp
from jax import lax

C = 128
K = 27
BLOCK = 128
BLK_DEV = 4
HB = 2
SCENES = 4
SLABS = 8
ROWS_DEV = 512
NROWS = 4096
NBLOCKS = 32
RULES = 256
HALO = 256
EXT = 1024


def draw_rules(key, part):
    total = SCENES * SLABS * K
    key_out, key_in, key_count = jax.random.split(key, 3)
    out_keys = jax.random.split(key_out, total)
    in_keys = jax.random.split(key_in, total)
    targets = jax.vmap(lambda kk: jax.random.permutation(kk, ROWS_DEV)[:RULES])(out_keys).astype(jnp.int32)
    sources = jax.vmap(lambda kk: jax.random.permutation(kk, EXT)[:RULES])(in_keys).astype(jnp.int32)
    counts = jax.random.randint(key_count, (total,), RULES // 2, RULES + 1).astype(jnp.int32)
    offset = jnp.arange(total, dtype=jnp.int32) % K
    centre = offset == K // 2
    counts = jnp.where(centre, RULES, counts)
    sources = jnp.where(centre[:, None], targets, sources)
    live = jnp.arange(RULES, dtype=jnp.int32)[None, :] < counts[:, None]
    targets = jnp.where(live, targets, ROWS_DEV)
    sources = jnp.where(live, sources, EXT)
    sources = sources.reshape(SCENES, SLABS, K, RULES)
    targets = targets.reshape(SCENES, SLABS, K, RULES)
    return jnp.stack([sources, targets], axis=2).astype(jnp.int32)


def place_ends(drawn, rng, smallest, top_value):
    place = [jax.random.randint(jax.random.fold_in(rng, axis), (), 0, length) for axis, length in enumerate(drawn.shape)]
    longest = drawn.shape.index(max(drawn.shape))
    neighbour = place[:longest] + [(place[longest] + 1) % drawn.shape[longest]] + place[longest + 1:]
    return drawn.at[tuple(place)].set(smallest).at[tuple(neighbour)].set(top_value)


def shard_levels(rng, dims, cuts, least, largest):
    def one(dim, parts):
        steps = jax.random.uniform(jax.random.fold_in(jax.random.fold_in(rng, 6), dim), (parts,), jnp.float32, least / len(cuts), largest / len(cuts))
        return jnp.repeat(jnp.exp(steps), dims[dim] // parts).reshape((-1,) + (1,) * (len(dims) - dim - 1))

    factor_of = one(*cuts[0])
    for cut in cuts[1:]:
        factor_of = factor_of * one(*cut)
    return factor_of


def noise(key, extent, spread, reach, cuts=(), kind=jnp.bfloat16):
    result = spread * jax.random.normal(key, extent, jnp.float32)
    if cuts:
        result = result * shard_levels(key, extent, cuts, -0.22, 0.18)
    return jnp.clip(result, -reach, reach).astype(kind)


def setup_inputs(seed: int = 0) -> dict:
    splits = jax.random.split(jax.random.key(seed), 8)
    return {
        "features": noise(splits[0], (SCENES, NROWS, C), 1.0, 6.0, ((0, 4), (1, 8))),
        "cotangent": noise(splits[1], (SCENES, NROWS, C), 1.0, 6.0, ((0, 4), (1, 8))),
        "weight_one": noise(splits[2], (K, C, C), (K * C // 4) ** -0.5, 0.21875),
        "weight_two": noise(splits[3], (K, C, C), (K * C // 4) ** -0.5, 0.21875),
        "rules": draw_rules(jax.random.fold_in(splits[7], 71), 0),
        "halo_send": place_ends(jax.random.randint(splits[5], (SCENES, SLABS, 2, HB), 0, BLK_DEV), jax.random.fold_in(splits[5], 1), 0, BLK_DEV - 1).astype(jnp.int32),
        "block_counts": place_ends(jax.random.randint(splits[6], (SCENES, NBLOCKS), BLOCK // 8, BLOCK + 1), jax.random.fold_in(splits[6], 1), BLOCK // 8, BLOCK).astype(jnp.int32),
    }


def mat_rows(gathered, weight):
    return jnp.einsum('krc,kcd->krd', gathered.astype(jnp.float32), weight.astype(jnp.float32), precision=lax.Precision.HIGHEST)

def mat_back(cot_rows, weight):
    return jnp.einsum('krd,kcd->krc', cot_rows.astype(jnp.float32), weight.astype(jnp.float32), precision=lax.Precision.HIGHEST)

def outer_sum(left, right):
    return jnp.einsum('krc,krd->kcd', left.astype(jnp.float32), right.astype(jnp.float32), precision=lax.Precision.HIGHEST)

def extend(table, send_rows):
    picked = jax.vmap(lambda t, idx: jnp.take(t, idx.reshape(-1), axis=0).reshape(2, HALO, C))(table, send_rows)
    zero_rim = jnp.zeros((1, HALO, C), table.dtype)
    from_left = jnp.concatenate([zero_rim, picked[:-1, 1]], axis=0)
    from_right = jnp.concatenate([picked[1:, 0], zero_rim], axis=0)
    zero_row = jnp.zeros((SLABS, 1, C), table.dtype)
    return jnp.concatenate([table, from_left, from_right, zero_row], axis=1)

def assemble(dext, send_rows):
    own = dext[:, :ROWS_DEV]
    grad_left = dext[:, ROWS_DEV:ROWS_DEV + HALO]
    grad_right = dext[:, ROWS_DEV + HALO:ROWS_DEV + 2 * HALO]
    zero_rim = jnp.zeros((1, HALO, C), jnp.float32)
    left_back = jnp.concatenate([zero_rim, grad_right[:-1]], axis=0)
    right_back = jnp.concatenate([grad_left[1:], zero_rim], axis=0)

    def add_back(rows_own, idx, first, second):
        return rows_own.at[idx[0]].add(first).at[idx[1]].add(second)
    return jax.vmap(add_back)(own, send_rows, left_back, right_back)

def reference(features, cotangent, weight_one, weight_two, rules, halo_send, block_counts):
    global_weights = jnp.stack([weight_one, weight_two])
    scene_fn = make_scene(global_weights)
    grad_rows, gw1, gw2 = lax.map(scene_fn, (features, cotangent, rules, halo_send, block_counts))
    scale = 1.0 / jnp.sqrt(jnp.float32(SCENES * SLABS * RULES))
    return (grad_rows, lax.optimization_barrier(jnp.sum(gw1, axis=0)) * scale, lax.optimization_barrier(jnp.sum(gw2, axis=0)) * scale)

def make_scene(weights):

    def scene_with(items):
        return scene_core(items, weights)
    return scene_with

def scene_core(items, weights):
    feats, cot, links, sends, counts = items
    active = (jnp.arange(BLOCK)[None, :] < counts[:, None]).astype(jnp.float32).reshape(SLABS, ROWS_DEV, 1)
    feats = feats.reshape(SLABS, ROWS_DEV, C)
    cot = cot.reshape(SLABS, ROWS_DEV, C)
    xa = feats * active.astype(jnp.bfloat16)
    ga = cot * active.astype(jnp.bfloat16)
    send_rows = (sends[:, :, :, None] * BLOCK + jnp.arange(BLOCK)[None, None, None, :]).reshape(SLABS, 2, HALO).astype(jnp.int32)
    ext_x = extend(xa, send_rows)
    weight_first = weights[0]
    weight_second = weights[1]

    def forward_slab(args):
        table, link = args
        prod = mat_rows(jnp.take(table, link[0], axis=0), weight_first)
        return jnp.zeros((ROWS_DEV + 1, C), jnp.float32).at[link[1].reshape(-1)].add(prod.reshape(-1, C))[:ROWS_DEV]
    z1 = lax.map(forward_slab, (ext_x, links))
    y1 = (jax.nn.silu(z1) * active).astype(jnp.bfloat16)
    ext_y = extend(y1, send_rows)

    def second_slab(args):
        table, cot_rows, link = args
        padded = jnp.concatenate([cot_rows, jnp.zeros((1, C), jnp.bfloat16)], axis=0)
        gga = jnp.take(padded, link[1], axis=0)
        gw = outer_sum(jnp.take(table, link[0], axis=0), gga)
        prod = mat_back(gga, weight_second)
        dext = jnp.zeros((EXT + 1, C), jnp.float32).at[link[0].reshape(-1)].add(prod.reshape(-1, C))
        return (gw, dext)
    gw2_slabs, dext_y = lax.map(second_slab, (ext_y, ga, links))
    dy1 = assemble(dext_y, send_rows)
    sig = jax.nn.sigmoid(z1)
    dz1 = (dy1 * sig * (1.0 + z1 * (1.0 - sig)) * active).astype(jnp.bfloat16)

    def first_slab(args):
        table, dz_rows, link = args
        padded = jnp.concatenate([dz_rows, jnp.zeros((1, C), jnp.bfloat16)], axis=0)
        dz_out = jnp.take(padded, link[1], axis=0)
        gw = outer_sum(jnp.take(table, link[0], axis=0), dz_out)
        prod = mat_back(dz_out, weight_first)
        dext = jnp.zeros((EXT + 1, C), jnp.float32).at[link[0].reshape(-1)].add(prod.reshape(-1, C))
        return (gw, dext)
    gw1_slabs, dext_x = lax.map(first_slab, (ext_x, dz1, links))
    grad_rows = assemble(dext_x, send_rows) * active
    return (grad_rows.reshape(NROWS, C), lax.optimization_barrier(jnp.sum(gw1_slabs, axis=0)), lax.optimization_barrier(jnp.sum(gw2_slabs, axis=0)))
```

```python
import functools

import jax
import jax.numpy as jnp
from jax import lax
from jax.experimental import pallas as pl
from jax.experimental.pallas import tpu as pltpu
from jax.sharding import PartitionSpec as P

F32 = jnp.float32
BF16 = jnp.bfloat16
CHUNK = 256
GROUP = 3
VMEM_LIMIT = 48 * 1024 * 1024


def dot(a, b):
    return jnp.dot(a, b, preferred_element_type=F32)


def dot_nt(a, b):
    return lax.dot_general(a, b, (((1,), (1,)), ((), ())), preferred_element_type=F32)


def dot_tn(a, b):
    return lax.dot_general(a, b, (((0,), (0,)), ((), ())), preferred_element_type=F32)


def one_hot(index_row, count):
    slots = index_row.shape[1]
    index = index_row.astype(F32)
    rows = lax.broadcasted_iota(jnp.int32, (CHUNK, slots), 0).astype(F32).astype(BF16)
    one, zero = jnp.ones((), BF16), jnp.zeros((), BF16)
    parts = []
    for base in range(0, count, CHUNK):
        shifted = jnp.broadcast_to((index - base).astype(BF16), (CHUNK, slots))
        parts.append(jnp.where(rows == shifted, one, zero))
    return jnp.concatenate(parts, axis=0)


def active_mask(counts_ref, blocks, block, width):
    lane = lax.broadcasted_iota(jnp.int32, (width, block), 1)
    return [(lane < counts_ref[0, b]).astype(F32) for b in range(blocks)]


def pick(sends_ref, side, per_side, table, blocks, block):
    picked = []
    for j in range(per_side):
        total = 0.0
        for b in range(blocks):
            total = total + jnp.where(
                sends_ref[side, j] == b, table[:, b * block : (b + 1) * block], 0.0
            )
        picked.append(total)
    return jnp.concatenate(picked, axis=1)


def add_back(own, sends_ref, per_side, from_left, from_right, blocks, block):
    out = []
    for b in range(blocks):
        total = own[:, b * block : (b + 1) * block]
        for side, back in ((0, from_left), (1, from_right)):
            for j in range(per_side):
                total = total + jnp.where(
                    sends_ref[side, j] == b, back[:, j * block : (j + 1) * block], 0.0
                )
        out.append(total)
    return jnp.concatenate(out, axis=1)


def prep_kernel(dims, feats, cot, counts, sends, xa_t, ga_t, low, high):
    blocks, block, per_side = dims
    width = feats.shape[1]
    mask = jnp.concatenate(active_mask(counts, blocks, block, width), axis=1)
    xa = feats[...].astype(F32).T * mask
    xa_t[...] = xa.astype(BF16)
    ga_t[...] = (cot[...].astype(F32).T * mask).astype(BF16)
    low[...] = pick(sends, 0, per_side, xa, blocks, block).astype(BF16)
    high[...] = pick(sends, 1, per_side, xa, blocks, block).astype(BF16)


def back_two_kernel(ga_t, rules, weight, dext, gga):
    width, rows = ga_t.shape
    ext_rows = dext.shape[1]
    kernels = weight.shape[0]
    dext[...] = jnp.zeros_like(dext)

    def step(i, _):
        weights, placed = [], []
        for j in range(GROUP):
            k = i * GROUP + j
            gathered = dot(ga_t[...], one_hot(rules[1, pl.ds(k, 1), :], rows)).astype(BF16)
            gga[k] = gathered
            placed.append(
                dot_nt(gathered, one_hot(rules[0, pl.ds(k, 1), :], ext_rows)).astype(BF16)
            )
            weights.append(weight[k])
        dext[...] += dot(jnp.concatenate(weights, axis=1), jnp.concatenate(placed, axis=0))
        return 0

    lax.fori_loop(0, kernels // GROUP, step, 0)


def forward_kernel(dims, xa_t, left, right, rules, weight, counts, sends, gx, y_t, slope, low, high, ext, z):
    blocks, block, per_side = dims
    width, rows = xa_t.shape
    halo = left.shape[1]
    ext_rows = ext.shape[1]
    kernels = weight.shape[0]
    ext[:, :rows] = xa_t[...]
    ext[:, rows : rows + halo] = left[...]
    ext[:, rows + halo :] = right[...]
    z[...] = jnp.zeros_like(z)

    def step(i, _):
        weights, placed = [], []
        for j in range(GROUP):
            k = i * GROUP + j
            gathered = dot(ext[...], one_hot(rules[0, pl.ds(k, 1), :], ext_rows)).astype(BF16)
            gx[k] = gathered
            placed.append(dot_nt(gathered, one_hot(rules[1, pl.ds(k, 1), :], rows)).astype(BF16))
            weights.append(weight[k])
        z[...] += dot_tn(jnp.concatenate(weights, axis=0), jnp.concatenate(placed, axis=0))
        return 0

    lax.fori_loop(0, kernels // GROUP, step, 0)
    mask = jnp.concatenate(active_mask(counts, blocks, block, width), axis=1)
    zv = z[...]
    sig = 1.0 / (1.0 + jnp.exp(-zv))
    y = ((zv * sig) * mask).astype(BF16)
    y_t[...] = y
    y32 = y.astype(F32)
    slope[...] = sig * (1.0 + zv * (1.0 - sig)) * mask
    low[...] = pick(sends, 0, per_side, y32, blocks, block).astype(BF16)
    high[...] = pick(sends, 1, per_side, y32, blocks, block).astype(BF16)


def back_one_kernel(dims, dext_y, back_left, back_right, slope, sends, rules, weight, gx, dext, grad, dz):
    blocks, block, per_side = dims
    width, rows = slope.shape
    ext_rows = dext.shape[1]
    kernels = weight.shape[0]
    dy = add_back(
        dext_y[:, :rows], sends, per_side, back_left[...], back_right[...], blocks, block
    )
    dz[...] = (dy * slope[...]).astype(BF16)
    dext[...] = jnp.zeros_like(dext)

    def step(i, _):
        products, selectors = [], []
        for j in range(GROUP):
            k = i * GROUP + j
            gathered = dot(dz[...], one_hot(rules[1, pl.ds(k, 1), :], rows)).astype(BF16)
            grad[k] = dot_nt(gx[k], gathered)
            products.append(dot(weight[k], gathered).astype(BF16))
            selectors.append(one_hot(rules[0, pl.ds(k, 1), :], ext_rows))
        dext[...] += dot_nt(jnp.concatenate(products, axis=1), jnp.concatenate(selectors, axis=1))
        return 0

    lax.fori_loop(0, kernels // GROUP, step, 0)


def grad_two_kernel(y_t, left, right, rules, gga, grad, ext):
    width, rows = y_t.shape
    halo = left.shape[1]
    ext_rows = ext.shape[1]
    kernels = gga.shape[0]
    ext[:, :rows] = y_t[...]
    ext[:, rows : rows + halo] = left[...]
    ext[:, rows + halo :] = right[...]

    def step(i, _):
        for j in range(GROUP):
            k = i * GROUP + j
            gathered = dot(ext[...], one_hot(rules[0, pl.ds(k, 1), :], ext_rows)).astype(BF16)
            grad[k] = dot_nt(gathered, gga[k])
        return 0

    lax.fori_loop(0, kernels // GROUP, step, 0)


def finish_kernel(dims, dext, back_left, back_right, counts, sends, out):
    blocks, block, per_side = dims
    rows, width = out.shape
    own = add_back(
        dext[:, :rows], sends, per_side, back_left[...], back_right[...], blocks, block
    )
    mask = jnp.concatenate(active_mask(counts, blocks, block, width), axis=1)
    out[...] = (own * mask).T


def call(kernel, kinds, outs, scratch=()):
    spaces = {"v": pltpu.VMEM, "s": pltpu.SMEM}
    return pl.pallas_call(
        kernel,
        out_shape=[jax.ShapeDtypeStruct(shape, dtype) for shape, dtype in outs],
        in_specs=[pl.BlockSpec(memory_space=spaces[kind]) for kind in kinds],
        out_specs=[pl.BlockSpec(memory_space=pltpu.VMEM) for _ in outs],
        scratch_shapes=list(scratch),
        compiler_params=pltpu.CompilerParams(vmem_limit_bytes=VMEM_LIMIT),
    )


def body(features, cotangent, weight_one, weight_two, rules, halo_send, block_counts):
    feats, cot, links, sends, counts = (
        features[0], cotangent[0], rules[0, 0], halo_send[0, 0], block_counts
    )
    rows, width = feats.shape
    blocks = counts.shape[1]
    block = rows // blocks
    per_side = sends.shape[1]
    halo = per_side * block
    kernels, slots = links.shape[1:]
    ext_rows = rows + 2 * halo
    dims = (blocks, block, per_side)
    count = lax.axis_size("space")
    up = [(i, i + 1) for i in range(count - 1)]
    down = [(t, s) for s, t in up]

    def swap(to_low, to_high):
        return lax.ppermute(to_high, "space", up), lax.ppermute(to_low, "space", down)

    xa_t, ga_t, x_low, x_high = call(
        functools.partial(prep_kernel, dims),
        "vvss",
        [((width, rows), BF16)] * 2 + [((width, halo), BF16)] * 2,
    )(feats, cot, counts, sends)
    x_left, x_right = swap(x_low, x_high)
    dext_y, gga = call(
        back_two_kernel,
        "vvv",
        [((width, ext_rows), F32), ((kernels, width, slots), BF16)],
    )(ga_t, links, weight_two)
    dy_left, dy_right = swap(dext_y[:, rows : rows + halo], dext_y[:, rows + halo :])
    gx, y_t, slope, y_low, y_high = call(
        functools.partial(forward_kernel, dims),
        "vvvvvss",
        [((kernels, width, slots), BF16), ((width, rows), BF16), ((width, rows), F32)]
        + [((width, halo), BF16)] * 2,
        [pltpu.VMEM((width, ext_rows), BF16), pltpu.VMEM((width, rows), F32)],
    )(xa_t, x_left, x_right, links, weight_one, counts, sends)
    y_left, y_right = swap(y_low, y_high)
    dext_x, grad_one = call(
        functools.partial(back_one_kernel, dims),
        "vvvvsvvv",
        [((width, ext_rows), F32), ((kernels, width, width), F32)],
        [pltpu.VMEM((width, rows), BF16)],
    )(dext_y, dy_left, dy_right, slope, sends, links, weight_one, gx)
    dx_left, dx_right = swap(dext_x[:, rows : rows + halo], dext_x[:, rows + halo :])
    total_one = lax.psum(grad_one, ("space", "dp"))
    (grad_two,) = call(
        grad_two_kernel,
        "vvvvv",
        [((kernels, width, width), F32)],
        [pltpu.VMEM((width, ext_rows), BF16)],
    )(y_t, y_left, y_right, links, gga)
    total_two = lax.psum(grad_two, ("space", "dp"))
    (grad_rows,) = call(
        functools.partial(finish_kernel, dims), "vvvss", [((rows, width), F32)]
    )(dext_x, dx_left, dx_right, counts, sends)
    scale = 1.0 / jnp.sqrt(F32(lax.axis_size("dp") * count * slots))
    return (grad_rows[None], total_one * scale, total_two * scale)


def solution(mesh):
    in_specs = (
        P("dp", "space", None),
        P("dp", "space", None),
        P(),
        P(),
        P("dp", "space", None, None, None),
        P("dp", "space", None, None),
        P("dp", "space"),
    )
    out_specs = (P("dp", "space", None), P(), P())
    return jax.shard_map(body, mesh=mesh, in_specs=in_specs, out_specs=out_specs, check_vma=False)
```

```python
import functools

import jax
import jax.numpy as jnp
from jax import lax
from jax.experimental import pallas as pl
from jax.experimental.pallas import tpu as pltpu
from jax.sharding import PartitionSpec as P

F32 = jnp.float32
BF16 = jnp.bfloat16
CHUNK = 256
GROUP = 3
VMEM_LIMIT = 48 * 1024 * 1024


def dot(a, b):
    return jnp.dot(a, b, preferred_element_type=F32)


def dot_nt(a, b):
    return lax.dot_general(a, b, (((1,), (1,)), ((), ())), preferred_element_type=F32)


def dot_tn(a, b):
    return lax.dot_general(a, b, (((0,), (0,)), ((), ())), preferred_element_type=F32)


def one_hot(index_row, count):
    slots = index_row.shape[1]
    index = index_row.astype(F32)
    rows = lax.broadcasted_iota(jnp.int32, (CHUNK, slots), 0).astype(F32).astype(BF16)
    one, zero = jnp.ones((), BF16), jnp.zeros((), BF16)
    parts = []
    for base in range(0, count, CHUNK):
        shifted = jnp.broadcast_to((index - base).astype(BF16), (CHUNK, slots))
        parts.append(jnp.where(rows == shifted, one, zero))
    return jnp.concatenate(parts, axis=0)


def active_mask(counts_ref, blocks, block, width):
    lane = lax.broadcasted_iota(jnp.int32, (width, block), 1)
    return [(lane < counts_ref[0, b]).astype(F32) for b in range(blocks)]


def pick(sends_ref, side, per_side, table, blocks, block):
    picked = []
    for j in range(per_side):
        total = 0.0
        for b in range(blocks):
            total = total + jnp.where(
                sends_ref[side, j] == b, table[:, b * block : (b + 1) * block], 0.0
            )
        picked.append(total)
    return jnp.concatenate(picked, axis=1)


def add_back(own, sends_ref, per_side, from_left, from_right, blocks, block):
    out = []
    for b in range(blocks):
        total = own[:, b * block : (b + 1) * block]
        for side, back in ((0, from_left), (1, from_right)):
            for j in range(per_side):
                total = total + jnp.where(
                    sends_ref[side, j] == b, back[:, j * block : (j + 1) * block], 0.0
                )
        out.append(total)
    return jnp.concatenate(out, axis=1)


class Exchange:
    def __init__(self, topo, local, land, half_own, half_send, land_quad, quad_send, land_line, out, send_sems, recv_sems):
        self.topo, self.local, self.land = topo, local, land
        self.half_own, self.half_send, self.land_quad = half_own, half_send, land_quad
        self.quad_send, self.land_line, self.out = quad_send, land_line, out
        self.send_sems, self.recv_sems = send_sems, recv_sems
        self.half = half_own.shape[0]
        self.quad = self.half // topo.n_quad
        self.piece = self.quad // topo.n_line
        self.next_sem = 0

    def copy(self, src, dst, device):
        sem = self.next_sem
        self.next_sem += 1
        return pltpu.make_async_remote_copy(
            src_ref=src,
            dst_ref=dst,
            send_sem=self.send_sems.at[sem],
            recv_sem=self.recv_sems.at[sem],
            device_id=device,
            device_id_type=pl.DeviceIdType.MESH,
        )

    def start(self, copies):
        for copy in copies:
            copy.start()
        self.flying = copies

    def land_all(self):
        for copy in self.flying:
            copy.wait()

    def stage_core(self):
        t = self.topo
        self.start([
            self.copy(self.local.at[pl.ds((1 - t.core) * self.half, self.half)], self.land, t.device(core=1 - t.core))
        ])

    def stage_quad(self):
        t = self.topo
        self.land_all()
        total = self.local[pl.ds(t.core * self.half, self.half)] + self.land[...]
        self.half_own[...] = total
        self.half_send[...] = total.astype(BF16)
        copies = []
        for d in range(1, t.n_quad):
            q = lax.rem(t.quad + d, t.n_quad)
            copies.append(self.copy(
                self.half_send.at[pl.ds(q * self.quad, self.quad)], self.land_quad.at[d - 1], t.device(quad=q)
            ))
        self.start(copies)

    def stage_line(self):
        t = self.topo
        self.land_all()
        total = self.half_own[pl.ds(t.quad * self.quad, self.quad)]
        for d in range(1, t.n_quad):
            total = total + self.land_quad[d - 1].astype(F32)
        self.half_own[pl.ds(t.quad * self.quad, self.quad)] = total
        self.quad_send[...] = total.astype(BF16)
        copies = []
        for d in range(1, t.n_line):
            w = lax.rem(t.line + d, t.n_line)
            copies.append(self.copy(
                self.quad_send.at[pl.ds(w * self.piece, self.piece)], self.land_line.at[d - 1], t.device(line=w)
            ))
        self.start(copies)

    def stage_share_line(self):
        t = self.topo
        self.land_all()
        total = self.half_own[pl.ds(t.quad * self.quad + t.line * self.piece, self.piece)]
        for d in range(1, t.n_line):
            total = total + self.land_line[d - 1].astype(F32)
        place = pl.ds(t.core * self.half + t.quad * self.quad + t.line * self.piece, self.piece)
        self.out[place] = total.astype(BF16)
        self.start([
            self.copy(self.out.at[place], self.out.at[place], t.device(line=lax.rem(t.line + d, t.n_line)))
            for d in range(1, t.n_line)
        ])

    def stage_share_quad(self):
        t = self.topo
        self.land_all()
        place = pl.ds(t.core * self.half + t.quad * self.quad, self.quad)
        self.start([
            self.copy(self.out.at[place], self.out.at[place], t.device(quad=lax.rem(t.quad + d, t.n_quad)))
            for d in range(1, t.n_quad)
        ])

    def stage_share_core(self):
        t = self.topo
        self.land_all()
        place = pl.ds(t.core * self.half, self.half)
        self.start([self.copy(self.out.at[place], self.out.at[place], t.device(core=1 - t.core))])


class Topology:
    def __init__(self, n_space, n_dp):
        self.n_space, self.n_dp = n_space, n_dp
        self.n_line = n_space // 2
        self.n_quad = (n_dp // 2) * 2
        self.space, self.dp = lax.axis_index("space"), lax.axis_index("dp")
        self.core = lax.rem(self.dp, 2)
        self.quad = (self.dp // 2) * 2 + lax.rem(self.space, 2)
        self.line = self.space // 2

    def device(self, core=None, quad=None, line=None):
        core = self.core if core is None else core
        quad = self.quad if quad is None else quad
        line = self.line if line is None else line
        return (line * 2 + lax.rem(quad, 2), (quad // 2) * 2 + core)

    def partners(self):
        found = [self.device(core=1 - self.core)]
        found += [self.device(quad=lax.rem(self.quad + d, self.n_quad)) for d in range(1, self.n_quad)]
        found += [self.device(line=lax.rem(self.line + d, self.n_line)) for d in range(1, self.n_line)]
        found += [(lax.rem(self.space + d, self.n_space), self.dp) for d in (1, self.n_space - 1)]
        return found


def exchange_copies(n_quad, n_line):
    return 2 * (1 + (n_quad - 1) + (n_line - 1))


def whole_kernel(
    dims, n_space, n_dp,
    feats, cot, weight_one, weight_two, rules, sends, counts,
    grad_rows, out_one, out_two,
    xa_t, ga_t, gga, gx, prod, ext, z, slope, dz, dext, dext_rim, rim_low, rim_high, rim32, halo_bf, halo_f32,
    local_one, local_two, land, half_own, half_send, land_quad, quad_send, land_line,
    send_sems, recv_sems, halo_send_sems, halo_recv_sems,
):
    blocks, block, per_side = dims
    rows, width = feats.shape
    halo = per_side * block
    ext_rows = rows + 2 * halo
    kernels, slots = rules.shape[1:]
    groups = kernels // GROUP
    topo = Topology(n_space, n_dp)
    barrier = pltpu.get_barrier_semaphore()
    partners = topo.partners()
    for device in partners:
        pl.semaphore_signal(barrier, inc=1, device_id=device, device_id_type=pl.DeviceIdType.MESH)

    mask = jnp.concatenate(active_mask(counts, blocks, block, width), axis=1)
    xa = feats[...].astype(F32).T * mask
    xa_t[...] = xa.astype(BF16)
    ga_t[...] = (cot[...].astype(F32).T * mask).astype(BF16)
    rim_low[0] = pick(sends, 0, per_side, xa, blocks, block).astype(BF16)
    rim_high[0] = pick(sends, 1, per_side, xa, blocks, block).astype(BF16)
    for s in range(2):
        @pl.when(topo.space == 0)
        def _():
            halo_bf[s, 0] = jnp.zeros((width, halo), BF16)
            halo_f32[s, 0] = jnp.zeros((width, halo), F32)

        @pl.when(topo.space == n_space - 1)
        def _():
            halo_bf[s, 1] = jnp.zeros((width, halo), BF16)
            halo_f32[s, 1] = jnp.zeros((width, halo), F32)

    per = width // 16
    pad = (local_one.shape[0] // per) - kernels
    for local in (local_one, local_two):
        if pad:
            local[pl.ds(kernels * per, pad * per)] = jnp.zeros((pad * per, 16, width), F32)
    pl.semaphore_wait(barrier, len(partners))

    def halo_copies(which, to_low, to_high, landing):
        def make(src, side, device):
            return pltpu.make_async_remote_copy(
                src_ref=src,
                dst_ref=landing.at[side],
                send_sem=halo_send_sems.at[which, side],
                recv_sem=halo_recv_sems.at[which, side],
                device_id=(device, topo.dp),
                device_id_type=pl.DeviceIdType.MESH,
            )
        up = make(to_high, 0, lax.rem(topo.space + 1, n_space))
        down = make(to_low, 1, lax.rem(topo.space + n_space - 1, n_space))
        return up, down

    def halo_start(copies):
        up, down = copies

        @pl.when(topo.space < n_space - 1)
        def _():
            up.start()

        @pl.when(topo.space > 0)
        def _():
            down.start()

    def halo_wait(copies):
        up, down = copies

        @pl.when(topo.space < n_space - 1)
        def _():
            up.wait_send()
            down.wait_recv()

        @pl.when(topo.space > 0)
        def _():
            down.wait_send()
            up.wait_recv()

    x_copies = halo_copies(0, rim_low.at[0], rim_high.at[0], halo_bf.at[0])
    halo_start(x_copies)

    dext[...] = jnp.zeros_like(dext)

    def back_two(i, _):
        weights, placed = [], []
        for j in range(GROUP):
            k = i * GROUP + j
            gathered = dot(ga_t[...], one_hot(rules[1, pl.ds(k, 1), :], rows)).astype(BF16)
            gga[k] = gathered
            placed.append(
                dot_nt(gathered, one_hot(rules[0, pl.ds(k, 1), :], ext_rows)).astype(BF16)
            )
            weights.append(weight_two[k])
        dext[...] += dot(jnp.concatenate(weights, axis=1), jnp.concatenate(placed, axis=0))
        return 0

    lax.fori_loop(0, groups, back_two, 0)
    dext_rim[0, 0] = dext[:, rows : rows + halo]
    dext_rim[0, 1] = dext[:, rows + halo :]
    dy_copies = halo_copies(1, dext_rim.at[0, 0], dext_rim.at[0, 1], halo_f32.at[0])
    halo_start(dy_copies)

    halo_wait(x_copies)
    ext[:, :rows] = xa_t[...]
    ext[:, rows : rows + halo] = halo_bf[0, 0]
    ext[:, rows + halo :] = halo_bf[0, 1]
    z[...] = jnp.zeros_like(z)

    def forward(i, _):
        weights, placed = [], []
        for j in range(GROUP):
            k = i * GROUP + j
            gathered = dot(ext[...], one_hot(rules[0, pl.ds(k, 1), :], ext_rows)).astype(BF16)
            gx[k] = gathered
            placed.append(dot_nt(gathered, one_hot(rules[1, pl.ds(k, 1), :], rows)).astype(BF16))
            weights.append(weight_one[k])
        z[...] += dot_tn(jnp.concatenate(weights, axis=0), jnp.concatenate(placed, axis=0))
        return 0

    lax.fori_loop(0, groups, forward, 0)
    zv = z[...]
    sig = 1.0 / (1.0 + jnp.exp(-zv))
    y = ((zv * sig) * mask).astype(BF16)
    slope[...] = sig * (1.0 + zv * (1.0 - sig)) * mask
    y32 = y.astype(F32)
    rim_low[1] = pick(sends, 0, per_side, y32, blocks, block).astype(BF16)
    rim_high[1] = pick(sends, 1, per_side, y32, blocks, block).astype(BF16)
    y_copies = halo_copies(2, rim_low.at[1], rim_high.at[1], halo_bf.at[1])
    halo_start(y_copies)
    ext[:, :rows] = y

    halo_wait(dy_copies)
    dy = add_back(
        dext[:, :rows], sends, per_side, halo_f32[0, 0], halo_f32[0, 1], blocks, block
    )
    dz[...] = (dy * slope[...]).astype(BF16)

    def grad_first(i, _):
        for j in range(GROUP):
            k = i * GROUP + j
            gathered = dot(dz[...], one_hot(rules[1, pl.ds(k, 1), :], rows)).astype(BF16)
            local_one[pl.ds(k * per, per)] = dot_nt(gx[k], gathered).reshape(per, 16, width)
            prod[k] = dot(weight_one[k], gathered).astype(BF16)
        return 0

    lax.fori_loop(0, groups, grad_first, 0)

    def exchange(side, local, out):
        return Exchange(
            topo, local, land.at[side], half_own.at[side], half_send.at[side], land_quad.at[side],
            quad_send.at[side], land_line.at[side], out, send_sems.at[side], recv_sems.at[side],
        )

    one = exchange(0, local_one, out_one)
    two = exchange(1, local_two, out_two)
    one.stage_core()

    halo_wait(y_copies)
    ext[:, rows : rows + halo] = halo_bf[1, 0]
    ext[:, rows + halo :] = halo_bf[1, 1]

    def grad_second(i, _):
        for j in range(GROUP):
            k = i * GROUP + j
            gathered = dot(ext[...], one_hot(rules[0, pl.ds(k, 1), :], ext_rows)).astype(BF16)
            local_two[pl.ds(k * per, per)] = dot_nt(gathered, gga[k]).reshape(per, 16, width)
        return 0

    cut = (2 * groups) // 3
    lax.fori_loop(0, cut, grad_second, 0)
    one.stage_quad()
    lax.fori_loop(cut, groups, grad_second, 0)
    two.stage_core()

    dext[...] = jnp.zeros_like(dext)

    def back_one(i, _):
        products, selectors = [], []
        for j in range(GROUP):
            k = i * GROUP + j
            products.append(prod[k])
            selectors.append(one_hot(rules[0, pl.ds(k, 1), :], ext_rows))
        dext[...] += dot_nt(jnp.concatenate(products, axis=1), jnp.concatenate(selectors, axis=1))
        return 0

    cut_a, cut_b = groups // 3, (2 * groups) // 3
    lax.fori_loop(0, cut_a, back_one, 0)
    two.stage_quad()
    one.stage_line()
    lax.fori_loop(cut_a, cut_b, back_one, 0)
    one.stage_share_line()
    lax.fori_loop(cut_b, groups, back_one, 0)
    dext_rim[1, 0] = dext[:, rows : rows + halo]
    dext_rim[1, 1] = dext[:, rows + halo :]
    dx_copies = halo_copies(3, dext_rim.at[1, 0], dext_rim.at[1, 1], halo_f32.at[1])
    halo_start(dx_copies)
    two.stage_line()
    one.stage_share_quad()
    halo_wait(dx_copies)
    own = add_back(
        dext[:, :rows], sends, per_side, halo_f32[1, 0], halo_f32[1, 1], blocks, block
    )
    grad_rows[...] = (own * mask).T
    two.stage_share_line()
    one.stage_share_core()
    two.stage_share_quad()
    one.land_all()
    two.stage_share_core()
    two.land_all()


def body(n_space, n_dp, features, cotangent, weight_one, weight_two, rules, halo_send, block_counts):
    feats, cot, links, sends = features[0], cotangent[0], rules[0, 0], halo_send[0, 0]
    rows, width = feats.shape
    blocks = block_counts.shape[1]
    block = rows // blocks
    per_side = sends.shape[1]
    halo = per_side * block
    kernels, slots = links.shape[1:]
    ext_rows = rows + 2 * halo
    per = width // 16
    devices = n_space * n_dp
    padded = kernels
    while (padded * per) % devices:
        padded += 1
    tiles = padded * per
    half = tiles // 2
    n_quad, n_line = (n_dp // 2) * 2, n_space // 2
    quad = half // n_quad
    piece = quad // n_line
    copies = exchange_copies(n_quad, n_line)
    v, s = pltpu.VMEM, pltpu.SMEM
    grad_rows, one, two = pl.pallas_call(
        functools.partial(whole_kernel, (blocks, block, per_side), n_space, n_dp),
        out_shape=[
            jax.ShapeDtypeStruct((rows, width), F32),
            jax.ShapeDtypeStruct((tiles, 16, width), BF16),
            jax.ShapeDtypeStruct((tiles, 16, width), BF16),
        ],
        in_specs=[pl.BlockSpec(memory_space=m) for m in (v, v, v, v, v, s, s)],
        out_specs=[pl.BlockSpec(memory_space=v)] * 3,
        scratch_shapes=[
            v((width, rows), BF16),
            v((width, rows), BF16),
            v((kernels, width, slots), BF16),
            v((kernels, width, slots), BF16),
            v((kernels, width, slots), BF16),
            v((width, ext_rows), BF16),
            v((width, rows), F32),
            v((width, rows), F32),
            v((width, rows), BF16),
            v((width, ext_rows), F32),
            v((2, 2, width, halo), F32),
            v((2, width, halo), BF16),
            v((2, width, halo), BF16),
            v((8, 128), F32),
            v((2, 2, width, halo), BF16),
            v((2, 2, width, halo), F32),
            v((tiles, 16, width), F32),
            v((tiles, 16, width), F32),
            v((2, half, 16, width), F32),
            v((2, half, 16, width), F32),
            v((2, half, 16, width), BF16),
            v((2, n_quad - 1, quad, 16, width), BF16),
            v((2, quad, 16, width), BF16),
            v((2, n_line - 1, piece, 16, width), BF16),
            pltpu.SemaphoreType.DMA((2, copies)),
            pltpu.SemaphoreType.DMA((2, copies)),
            pltpu.SemaphoreType.DMA((4, 2)),
            pltpu.SemaphoreType.DMA((4, 2)),
        ],
        compiler_params=pltpu.CompilerParams(
            collective_id=0, has_side_effects=True, vmem_limit_bytes=VMEM_LIMIT
        ),
    )(feats, cot, weight_one, weight_two, links, sends, block_counts)
    scale = 1.0 / jnp.sqrt(F32(devices * slots))

    def finish(total):
        return total[: kernels * per].astype(F32).reshape(kernels, width, width) * scale

    return (grad_rows[None], finish(one), finish(two))


def solution(mesh):
    n_space, n_dp = mesh.shape["space"], mesh.shape["dp"]
    in_specs = (
        P("dp", "space", None),
        P("dp", "space", None),
        P(),
        P(),
        P("dp", "space", None, None, None),
        P("dp", "space", None, None),
        P("dp", "space"),
    )
    out_specs = (P("dp", "space", None), P(), P())
    return jax.shard_map(
        functools.partial(body, n_space, n_dp), mesh=mesh, in_specs=in_specs, out_specs=out_specs, check_vma=False)
```

```python
import functools

import jax
import jax.numpy as jnp
from jax import lax
from jax.experimental import pallas as pl
from jax.experimental.pallas import tpu as pltpu
from jax.sharding import PartitionSpec as P

F32 = jnp.float32
BF16 = jnp.bfloat16
CHUNK = 256
GROUP = 3
VMEM_LIMIT = 48 * 1024 * 1024


def dot(a, b):
    return jnp.dot(a, b, preferred_element_type=F32)


def dot_nt(a, b):
    return lax.dot_general(a, b, (((1,), (1,)), ((), ())), preferred_element_type=F32)


def dot_tn(a, b):
    return lax.dot_general(a, b, (((0,), (0,)), ((), ())), preferred_element_type=F32)


def one_hot(low_row):
    slots = low_row.shape[1]
    place = lax.broadcasted_iota(jnp.int32, (CHUNK, slots), 0).astype(F32).astype(BF16)
    return jnp.where(
        place == jnp.broadcast_to(low_row.astype(BF16), (CHUNK, slots)),
        jnp.ones((), BF16), jnp.zeros((), BF16),
    )


def gather(table, selector, chunk_row, width):
    found = dot(table, selector)
    chunks = table.shape[0] // width
    chunk = jnp.broadcast_to(chunk_row, (width, chunk_row.shape[1]))
    out = found[:width]
    for c in range(1, chunks):
        out = jnp.where(chunk == c, found[c * width : (c + 1) * width], out)
    return out.astype(BF16)


def spread(values, chunk_row, chunks):
    chunk = jnp.broadcast_to(chunk_row.astype(BF16), values.shape)
    zero = jnp.zeros((), BF16)
    return jnp.concatenate(
        [jnp.where(chunk == jnp.asarray(c, BF16), values, zero) for c in range(chunks)], axis=0
    )


def stack(table):
    return jnp.concatenate(
        [table[:, c : c + CHUNK] for c in range(0, table.shape[1], CHUNK)], axis=0
    )


def unstack(table, width):
    return jnp.concatenate(
        [table[r : r + width] for r in range(0, table.shape[0], width)], axis=1
    )


def active_mask(counts_ref, blocks, block, width):
    lane = lax.broadcasted_iota(jnp.int32, (width, block), 1)
    return [(lane < counts_ref[0, b]).astype(F32) for b in range(blocks)]


def pick(sends_ref, side, per_side, table, blocks, block):
    picked = []
    for j in range(per_side):
        total = 0.0
        for b in range(blocks):
            total = total + jnp.where(
                sends_ref[side, j] == b, table[:, b * block : (b + 1) * block], 0.0
            )
        picked.append(total)
    return jnp.concatenate(picked, axis=1)


def add_back(own, sends_ref, per_side, from_left, from_right, blocks, block):
    out = []
    for b in range(blocks):
        total = own[:, b * block : (b + 1) * block]
        for side, back in ((0, from_left), (1, from_right)):
            for j in range(per_side):
                total = total + jnp.where(
                    sends_ref[side, j] == b, back[:, j * block : (j + 1) * block], 0.0
                )
        out.append(total)
    return jnp.concatenate(out, axis=1)


class Exchange:
    def __init__(self, topo, local, land, half_own, half_send, land_quad, quad_send, land_line, out, send_sems, recv_sems):
        self.topo, self.local, self.land = topo, local, land
        self.half_own, self.half_send, self.land_quad = half_own, half_send, land_quad
        self.quad_send, self.land_line, self.out = quad_send, land_line, out
        self.send_sems, self.recv_sems = send_sems, recv_sems
        self.half = half_own.shape[0]
        self.quad = self.half // topo.n_quad
        self.piece = self.quad // topo.n_line
        self.next_sem = 0

    def copy(self, src, dst, device):
        sem = self.next_sem
        self.next_sem += 1
        return pltpu.make_async_remote_copy(
            src_ref=src,
            dst_ref=dst,
            send_sem=self.send_sems.at[sem],
            recv_sem=self.recv_sems.at[sem],
            device_id=device,
            device_id_type=pl.DeviceIdType.MESH,
        )

    def start(self, copies):
        for copy in copies:
            copy.start()
        self.flying = copies

    def land_all(self):
        for copy in self.flying:
            copy.wait()

    def stage_core(self):
        t = self.topo
        self.start([
            self.copy(self.local.at[pl.ds((1 - t.core) * self.half, self.half)], self.land, t.device(core=1 - t.core))
        ])

    def stage_quad(self):
        t = self.topo
        self.land_all()
        total = self.local[pl.ds(t.core * self.half, self.half)] + self.land[...]
        self.half_own[...] = total
        self.half_send[...] = total.astype(BF16)
        copies = []
        for d in range(1, t.n_quad):
            q = lax.rem(t.quad + d, t.n_quad)
            copies.append(self.copy(
                self.half_send.at[pl.ds(q * self.quad, self.quad)], self.land_quad.at[d - 1], t.device(quad=q)
            ))
        self.start(copies)

    def stage_line(self):
        t = self.topo
        self.land_all()
        total = self.half_own[pl.ds(t.quad * self.quad, self.quad)]
        for d in range(1, t.n_quad):
            total = total + self.land_quad[d - 1].astype(F32)
        self.half_own[pl.ds(t.quad * self.quad, self.quad)] = total
        self.quad_send[...] = total.astype(BF16)
        copies = []
        for d in range(1, t.n_line):
            w = lax.rem(t.line + d, t.n_line)
            copies.append(self.copy(
                self.quad_send.at[pl.ds(w * self.piece, self.piece)], self.land_line.at[d - 1], t.device(line=w)
            ))
        self.start(copies)

    def stage_share_line(self):
        t = self.topo
        self.land_all()
        total = self.half_own[pl.ds(t.quad * self.quad + t.line * self.piece, self.piece)]
        for d in range(1, t.n_line):
            total = total + self.land_line[d - 1].astype(F32)
        place = pl.ds(t.core * self.half + t.quad * self.quad + t.line * self.piece, self.piece)
        self.out[place] = total.astype(BF16)
        self.start([
            self.copy(self.out.at[place], self.out.at[place], t.device(line=lax.rem(t.line + d, t.n_line)))
            for d in range(1, t.n_line)
        ])

    def stage_share_quad(self):
        t = self.topo
        self.land_all()
        place = pl.ds(t.core * self.half + t.quad * self.quad, self.quad)
        self.start([
            self.copy(self.out.at[place], self.out.at[place], t.device(quad=lax.rem(t.quad + d, t.n_quad)))
            for d in range(1, t.n_quad)
        ])

    def stage_share_core(self):
        t = self.topo
        self.land_all()
        place = pl.ds(t.core * self.half, self.half)
        self.start([self.copy(self.out.at[place], self.out.at[place], t.device(core=1 - t.core))])


class Topology:
    def __init__(self, n_space, n_dp):
        self.n_space, self.n_dp = n_space, n_dp
        self.n_line = n_space // 2
        self.n_quad = (n_dp // 2) * 2
        self.space, self.dp = lax.axis_index("space"), lax.axis_index("dp")
        self.core = lax.rem(self.dp, 2)
        self.quad = (self.dp // 2) * 2 + lax.rem(self.space, 2)
        self.line = self.space // 2

    def device(self, core=None, quad=None, line=None):
        core = self.core if core is None else core
        quad = self.quad if quad is None else quad
        line = self.line if line is None else line
        return (line * 2 + lax.rem(quad, 2), (quad // 2) * 2 + core)

    def partners(self):
        found = [self.device(core=1 - self.core)]
        found += [self.device(quad=lax.rem(self.quad + d, self.n_quad)) for d in range(1, self.n_quad)]
        found += [self.device(line=lax.rem(self.line + d, self.n_line)) for d in range(1, self.n_line)]
        found += [(lax.rem(self.space + d, self.n_space), self.dp) for d in (1, self.n_space - 1)]
        return found


def exchange_copies(n_quad, n_line):
    return 2 * (1 + (n_quad - 1) + (n_line - 1))


def whole_kernel(
    dims, n_space, n_dp,
    feats, cot, weight_one, weight_two, rules, sends, counts,
    grad_rows, out_one, out_two,
    xa_t, ga_t, gga, gx, prod, ext, z, slope, dz, dext, dext_rim, rim_low, rim_high, rim32, halo_bf, halo_f32, low_rows, chunk_rows,
    local_one, local_two, land, half_own, half_send, land_quad, quad_send, land_line,
    send_sems, recv_sems, halo_send_sems, halo_recv_sems,
):
    blocks, block, per_side = dims
    rows, width = feats.shape
    halo = per_side * block
    ext_rows = rows + 2 * halo
    kernels, slots = rules.shape[1:]
    groups = kernels // GROUP
    own_chunks, ext_chunks = rows // CHUNK, ext_rows // CHUNK

    def selector(kind, k):
        return one_hot(low_rows[kind, pl.ds(k, 1), :])

    def chunk_of(kind, k):
        return chunk_rows[kind, pl.ds(k, 1), :]

    def own_part(ref):
        return unstack(ref[pl.ds(0, own_chunks * width)], width)

    def rim_part(ref, side):
        size = (halo // CHUNK) * width
        return unstack(ref[pl.ds(own_chunks * width + side * size, size)], width)

    def set_rim(ref, side, value):
        size = (halo // CHUNK) * width
        ref[pl.ds(own_chunks * width + side * size, size)] = stack(value)

    topo = Topology(n_space, n_dp)
    barrier = pltpu.get_barrier_semaphore()
    partners = topo.partners()
    for device in partners:
        pl.semaphore_signal(barrier, inc=1, device_id=device, device_id_type=pl.DeviceIdType.MESH)

    mask = jnp.concatenate(active_mask(counts, blocks, block, width), axis=1)
    for kind, limit in ((0, ext_rows), (1, rows)):
        index = rules[kind]
        low_rows[kind] = jnp.where(index < limit, lax.rem(index, CHUNK), -1).astype(F32)
        chunk_rows[kind] = (index // CHUNK).astype(F32)
    xa = feats[...].astype(F32).T * mask
    xa_t[...] = stack(xa.astype(BF16))
    ga_t[...] = stack((cot[...].astype(F32).T * mask).astype(BF16))
    rim_low[0] = pick(sends, 0, per_side, xa, blocks, block).astype(BF16)
    rim_high[0] = pick(sends, 1, per_side, xa, blocks, block).astype(BF16)
    for s in range(2):
        @pl.when(topo.space == 0)
        def _():
            halo_bf[s, 0] = jnp.zeros((width, halo), BF16)
            halo_f32[s, 0] = jnp.zeros((width, halo), F32)

        @pl.when(topo.space == n_space - 1)
        def _():
            halo_bf[s, 1] = jnp.zeros((width, halo), BF16)
            halo_f32[s, 1] = jnp.zeros((width, halo), F32)

    per = width // 16
    pad = (local_one.shape[0] // per) - kernels
    for local in (local_one, local_two):
        if pad:
            local[pl.ds(kernels * per, pad * per)] = jnp.zeros((pad * per, 16, width), F32)
    pl.semaphore_wait(barrier, len(partners))

    def halo_copies(which, to_low, to_high, landing):
        def make(src, side, device):
            return pltpu.make_async_remote_copy(
                src_ref=src,
                dst_ref=landing.at[side],
                send_sem=halo_send_sems.at[which, side],
                recv_sem=halo_recv_sems.at[which, side],
                device_id=(device, topo.dp),
                device_id_type=pl.DeviceIdType.MESH,
            )
        up = make(to_high, 0, lax.rem(topo.space + 1, n_space))
        down = make(to_low, 1, lax.rem(topo.space + n_space - 1, n_space))
        return up, down

    def halo_start(copies):
        up, down = copies

        @pl.when(topo.space < n_space - 1)
        def _():
            up.start()

        @pl.when(topo.space > 0)
        def _():
            down.start()

    def halo_wait(copies):
        up, down = copies

        @pl.when(topo.space < n_space - 1)
        def _():
            up.wait_send()
            down.wait_recv()

        @pl.when(topo.space > 0)
        def _():
            down.wait_send()
            up.wait_recv()

    x_copies = halo_copies(0, rim_low.at[0], rim_high.at[0], halo_bf.at[0])
    halo_start(x_copies)

    dext[...] = jnp.zeros_like(dext)

    def back_two(i, _):
        weights, placed = [], []
        for j in range(GROUP):
            k = i * GROUP + j
            found = gather(ga_t[...], selector(1, k), chunk_of(1, k), width)
            gga[k] = found
            placed.append(
                dot_nt(spread(found, chunk_of(0, k), ext_chunks), selector(0, k)).astype(BF16)
            )
            weights.append(weight_two[k])
        weights = jnp.concatenate(weights, axis=1)
        for c in range(ext_chunks):
            part = slice(c * width, (c + 1) * width)
            dext[part] += dot(weights, jnp.concatenate([p[part] for p in placed], axis=0))
        return 0

    lax.fori_loop(0, groups, back_two, 0)
    dext_rim[0, 0] = rim_part(dext, 0)
    dext_rim[0, 1] = rim_part(dext, 1)
    dy_copies = halo_copies(1, dext_rim.at[0, 0], dext_rim.at[0, 1], halo_f32.at[0])
    halo_start(dy_copies)

    halo_wait(x_copies)
    ext[pl.ds(0, own_chunks * width)] = xa_t[...]
    set_rim(ext, 0, halo_bf[0, 0])
    set_rim(ext, 1, halo_bf[0, 1])
    z[...] = jnp.zeros_like(z)

    def forward(i, _):
        weights, placed = [], []
        for j in range(GROUP):
            k = i * GROUP + j
            found = gather(ext[...], selector(0, k), chunk_of(0, k), width)
            gx[k] = found
            placed.append(
                dot_nt(spread(found, chunk_of(1, k), own_chunks), selector(1, k)).astype(BF16)
            )
            weights.append(weight_one[k])
        weights = jnp.concatenate(weights, axis=0)
        for c in range(own_chunks):
            part = slice(c * width, (c + 1) * width)
            z[part] += dot_tn(weights, jnp.concatenate([p[part] for p in placed], axis=0))
        return 0

    lax.fori_loop(0, groups, forward, 0)
    zv = unstack(z[...], width)
    sig = 1.0 / (1.0 + jnp.exp(-zv))
    y = ((zv * sig) * mask).astype(BF16)
    slope[...] = sig * (1.0 + zv * (1.0 - sig)) * mask
    y32 = y.astype(F32)
    rim_low[1] = pick(sends, 0, per_side, y32, blocks, block).astype(BF16)
    rim_high[1] = pick(sends, 1, per_side, y32, blocks, block).astype(BF16)
    y_copies = halo_copies(2, rim_low.at[1], rim_high.at[1], halo_bf.at[1])
    halo_start(y_copies)
    ext[pl.ds(0, own_chunks * width)] = stack(y)

    halo_wait(dy_copies)
    dy = add_back(
        own_part(dext), sends, per_side, halo_f32[0, 0], halo_f32[0, 1], blocks, block
    )
    dz[...] = stack((dy * slope[...]).astype(BF16))

    def grad_first(i, _):
        for j in range(GROUP):
            k = i * GROUP + j
            gathered = gather(dz[...], selector(1, k), chunk_of(1, k), width)
            local_one[pl.ds(k * per, per)] = dot_nt(gx[k], gathered).reshape(per, 16, width)
            prod[k] = dot(weight_one[k], gathered).astype(BF16)
        return 0

    lax.fori_loop(0, groups, grad_first, 0)

    def exchange(side, local, out):
        return Exchange(
            topo, local, land.at[side], half_own.at[side], half_send.at[side], land_quad.at[side],
            quad_send.at[side], land_line.at[side], out, send_sems.at[side], recv_sems.at[side],
        )

    one = exchange(0, local_one, out_one)
    two = exchange(1, local_two, out_two)
    one.stage_core()

    halo_wait(y_copies)
    set_rim(ext, 0, halo_bf[1, 0])
    set_rim(ext, 1, halo_bf[1, 1])

    def grad_second(i, _):
        for j in range(GROUP):
            k = i * GROUP + j
            gathered = gather(ext[...], selector(0, k), chunk_of(0, k), width)
            local_two[pl.ds(k * per, per)] = dot_nt(gathered, gga[k]).reshape(per, 16, width)
        return 0

    cut = (2 * groups) // 3
    lax.fori_loop(0, cut, grad_second, 0)
    one.stage_quad()
    lax.fori_loop(cut, groups, grad_second, 0)
    two.stage_core()

    dext[...] = jnp.zeros_like(dext)

    def back_one(i, _):
        products, selectors = [], []
        for j in range(GROUP):
            k = i * GROUP + j
            products.append(spread(prod[k], chunk_of(0, k), ext_chunks))
            selectors.append(selector(0, k))
        dext[...] += dot_nt(jnp.concatenate(products, axis=1), jnp.concatenate(selectors, axis=1))
        return 0

    cut_a, cut_b = groups // 3, (2 * groups) // 3
    lax.fori_loop(0, cut_a, back_one, 0)
    two.stage_quad()
    one.stage_line()
    lax.fori_loop(cut_a, cut_b, back_one, 0)
    one.stage_share_line()
    lax.fori_loop(cut_b, groups, back_one, 0)
    dext_rim[1, 0] = rim_part(dext, 0)
    dext_rim[1, 1] = rim_part(dext, 1)
    dx_copies = halo_copies(3, dext_rim.at[1, 0], dext_rim.at[1, 1], halo_f32.at[1])
    halo_start(dx_copies)
    two.stage_line()
    one.stage_share_quad()
    halo_wait(dx_copies)
    own = add_back(
        own_part(dext), sends, per_side, halo_f32[1, 0], halo_f32[1, 1], blocks, block
    )
    grad_rows[...] = (own * mask).T
    two.stage_share_line()
    one.stage_share_core()
    two.stage_share_quad()
    one.land_all()
    two.stage_share_core()
    two.land_all()


def body(n_space, n_dp, features, cotangent, weight_one, weight_two, rules, halo_send, block_counts):
    feats, cot, links, sends = features[0], cotangent[0], rules[0, 0], halo_send[0, 0]
    rows, width = feats.shape
    blocks = block_counts.shape[1]
    block = rows // blocks
    per_side = sends.shape[1]
    halo = per_side * block
    kernels, slots = links.shape[1:]
    ext_rows = rows + 2 * halo
    per = width // 16
    devices = n_space * n_dp
    padded = kernels
    while (padded * per) % devices:
        padded += 1
    tiles = padded * per
    half = tiles // 2
    n_quad, n_line = (n_dp // 2) * 2, n_space // 2
    quad = half // n_quad
    piece = quad // n_line
    copies = exchange_copies(n_quad, n_line)
    v, s = pltpu.VMEM, pltpu.SMEM
    grad_rows, one, two = pl.pallas_call(
        functools.partial(whole_kernel, (blocks, block, per_side), n_space, n_dp),
        out_shape=[
            jax.ShapeDtypeStruct((rows, width), F32),
            jax.ShapeDtypeStruct((tiles, 16, width), BF16),
            jax.ShapeDtypeStruct((tiles, 16, width), BF16),
        ],
        in_specs=[pl.BlockSpec(memory_space=m) for m in (v, v, v, v, v, s, s)],
        out_specs=[pl.BlockSpec(memory_space=v)] * 3,
        scratch_shapes=[
            v((width * rows // CHUNK, CHUNK), BF16),
            v((width * rows // CHUNK, CHUNK), BF16),
            v((kernels, width, slots), BF16),
            v((kernels, width, slots), BF16),
            v((kernels, width, slots), BF16),
            v((width * ext_rows // CHUNK, CHUNK), BF16),
            v((width * rows // CHUNK, CHUNK), F32),
            v((width, rows), F32),
            v((width * rows // CHUNK, CHUNK), BF16),
            v((width * ext_rows // CHUNK, CHUNK), F32),
            v((2, 2, width, halo), F32),
            v((2, width, halo), BF16),
            v((2, width, halo), BF16),
            v((8, 128), F32),
            v((2, 2, width, halo), BF16),
            v((2, 2, width, halo), F32),
            v((2, kernels, slots), F32),
            v((2, kernels, slots), F32),
            v((tiles, 16, width), F32),
            v((tiles, 16, width), F32),
            v((2, half, 16, width), F32),
            v((2, half, 16, width), F32),
            v((2, half, 16, width), BF16),
            v((2, n_quad - 1, quad, 16, width), BF16),
            v((2, quad, 16, width), BF16),
            v((2, n_line - 1, piece, 16, width), BF16),
            pltpu.SemaphoreType.DMA((2, copies)),
            pltpu.SemaphoreType.DMA((2, copies)),
            pltpu.SemaphoreType.DMA((4, 2)),
            pltpu.SemaphoreType.DMA((4, 2)),
        ],
        compiler_params=pltpu.CompilerParams(
            collective_id=0, has_side_effects=True, vmem_limit_bytes=VMEM_LIMIT
        ),
    )(feats, cot, weight_one, weight_two, links, sends, block_counts)
    scale = 1.0 / jnp.sqrt(F32(devices * slots))

    def finish(total):
        return total[: kernels * per].astype(F32).reshape(kernels, width, width) * scale

    return (grad_rows[None], finish(one), finish(two))


def solution(mesh):
    n_space, n_dp = mesh.shape["space"], mesh.shape["dp"]
    in_specs = (
        P("dp", "space", None),
        P("dp", "space", None),
        P(),
        P(),
        P("dp", "space", None, None, None),
        P("dp", "space", None, None),
        P("dp", "space"),
    )
    out_specs = (P("dp", "space", None), P(), P())
    return jax.shard_map(
        functools.partial(body, n_space, n_dp), mesh=mesh, in_specs=in_specs, out_specs=out_specs, check_vma=False)
```

```python
import functools

import jax
import jax.numpy as jnp
from jax import lax
from jax.experimental import pallas as pl
from jax.experimental.pallas import tpu as pltpu
from jax.sharding import PartitionSpec as P

F32 = jnp.float32
BF16 = jnp.bfloat16
CHUNK = 256
GROUP = 3
VMEM_LIMIT = 62 * 1024 * 1024


def dot(a, b):
    return jnp.dot(a, b, preferred_element_type=F32)


def dot_nt(a, b):
    return lax.dot_general(a, b, (((1,), (1,)), ((), ())), preferred_element_type=F32)


def dot_tn(a, b):
    return lax.dot_general(a, b, (((0,), (0,)), ((), ())), preferred_element_type=F32)


def one_hot(low_row):
    slots = low_row.shape[1]
    place = lax.broadcasted_iota(jnp.int32, (CHUNK, slots), 0).astype(F32).astype(BF16)
    return jnp.where(
        place == jnp.broadcast_to(low_row.astype(BF16), (CHUNK, slots)),
        jnp.ones((), BF16), jnp.zeros((), BF16),
    )


def gather(table, selector, chunk_row, width):
    found = dot(table, selector)
    chunks = table.shape[0] // width
    chunk = jnp.broadcast_to(chunk_row, (width, chunk_row.shape[1]))
    out = found[:width]
    for c in range(1, chunks):
        out = jnp.where(chunk == c, found[c * width : (c + 1) * width], out)
    return out.astype(BF16)


def spread(values, chunk_row, chunks):
    chunk = jnp.broadcast_to(chunk_row.astype(BF16), values.shape)
    zero = jnp.zeros((), BF16)
    return jnp.concatenate(
        [jnp.where(chunk == jnp.asarray(c, BF16), values, zero) for c in range(chunks)], axis=0
    )


def stack(table):
    return jnp.concatenate(
        [table[:, c : c + CHUNK] for c in range(0, table.shape[1], CHUNK)], axis=0
    )


def unstack(table, width):
    return jnp.concatenate(
        [table[r : r + width] for r in range(0, table.shape[0], width)], axis=1
    )


def active_mask(counts_ref, blocks, block, width):
    lane = lax.broadcasted_iota(jnp.int32, (width, block), 1)
    return [(lane < counts_ref[0, b]).astype(F32) for b in range(blocks)]


def pick(sends_ref, side, per_side, table, blocks, block):
    picked = []
    for j in range(per_side):
        total = 0.0
        for b in range(blocks):
            total = total + jnp.where(
                sends_ref[side, j] == b, table[:, b * block : (b + 1) * block], 0.0
            )
        picked.append(total)
    return jnp.concatenate(picked, axis=1)


def add_back(own, sends_ref, per_side, from_left, from_right, blocks, block):
    out = []
    for b in range(blocks):
        total = own[:, b * block : (b + 1) * block]
        for side, back in ((0, from_left), (1, from_right)):
            for j in range(per_side):
                total = total + jnp.where(
                    sends_ref[side, j] == b, back[:, j * block : (j + 1) * block], 0.0
                )
        out.append(total)
    return jnp.concatenate(out, axis=1)


class Topology:
    def __init__(self, n_space, n_dp):
        self.n_space, self.n_dp = n_space, n_dp
        self.size = {"core": 2, "side": 2, "rank": n_dp // 2, "line": n_space // 2}
        self.space, self.dp = lax.axis_index("space"), lax.axis_index("dp")
        self.at = {
            "core": lax.rem(self.dp, 2), "side": lax.rem(self.space, 2),
            "rank": self.dp // 2, "line": self.space // 2,
        }

    def others(self, axis):
        found = []
        for d in range(1, self.size[axis]):
            index = lax.rem(self.at[axis] + d, self.size[axis])
            at = dict(self.at, **{axis: index})
            found.append((d - 1, index, (at["line"] * 2 + at["side"], at["rank"] * 2 + at["core"])))
        return found

    def partners(self):
        found = [device for axis in self.size for _, _, device in self.others(axis)]
        found += [(lax.rem(self.space + d, self.n_space), self.dp) for d in (1, self.n_space - 1)]
        return found


class Exchange:
    def __init__(self, topo, axes, base, local, out, lands, sends, send_sems, recv_sems):
        self.topo, self.axes, self.local, self.out = topo, axes, local, out
        self.lands, self.sends, self.send_sems, self.recv_sems = lands, sends, send_sems, recv_sems
        self.offset, self.count = base, lands[0].shape[1] * topo.size[axes[0]]
        self.level, self.sem, self.flying, self.stack = 0, 0, [], []

    def copy(self, src, dst, device):
        sem, self.sem = self.sem, self.sem + 1
        made = pltpu.make_async_remote_copy(
            src_ref=src, dst_ref=dst, send_sem=self.send_sems.at[sem], recv_sem=self.recv_sems.at[sem],
            device_id=device, device_id_type=pl.DeviceIdType.MESH,
        )
        made.start()
        self.flying.append(made)

    def advance(self):
        for made in self.flying:
            made.wait()
        self.flying = []
        t, depth = self.topo, len(self.axes)
        if 0 < self.level <= depth:
            axis = self.axes[self.level - 1]
            self.stack.append((self.offset, self.count))
            self.count //= t.size[axis]
            self.offset = self.offset + t.at[axis] * self.count
            own = pl.ds(self.offset, self.count)
            total = self.local[own]
            for slot in range(t.size[axis] - 1):
                total = total + self.lands[self.level - 1][slot].astype(F32)
            if self.level < depth:
                self.local[own] = total
                self.sends[self.level - 1][...] = total.astype(BF16)
            else:
                self.out[own] = total.astype(BF16)
        if self.level < depth:
            axis = self.axes[self.level]
            piece = self.count // t.size[axis]
            for slot, index, device in t.others(axis):
                if self.level == 0:
                    src = self.local.at[pl.ds(self.offset + index * piece, piece)]
                else:
                    src = self.sends[self.level - 1].at[pl.ds(index * piece, piece)]
                self.copy(src, self.lands[self.level].at[slot], device)
        elif self.level < 2 * depth:
            axis = self.axes[2 * depth - 1 - self.level]
            place = self.out.at[pl.ds(self.offset, self.count)]
            for _, _, device in t.others(axis):
                self.copy(place, place, device)
            self.offset, self.count = self.stack.pop()
        self.level += 1


def plan_parts(n_space, n_dp, kernels, per):
    devices = n_space * n_dp
    units = -(-kernels * per // devices)
    first = (units + 1) // 2
    parts = [(0, first * devices, ("core", "side", "rank", "line"))]
    if units > first:
        parts.append((first * devices, (units - first) * devices, ("core", "rank", "side", "line")))
    return parts, units * devices


def part_shapes(sizes, tiles, axes, width):
    lands, sends = [], []
    for level, axis in enumerate(axes):
        if level:
            sends.append(pltpu.VMEM((tiles, 16, width), BF16))
        tiles //= sizes[axis]
        lands.append(pltpu.VMEM((sizes[axis] - 1, tiles, 16, width), BF16 if level else F32))
    return lands, sends


def whole_kernel(
    dims, n_space, n_dp,
    feats_hbm, cot_hbm, one_hbm, two_hbm, rules_hbm, sends_hbm, counts_hbm,
    grad_rows, out_one, out_two,
    feats, cot, weight_one, weight_two, rules, sends, counts, load_sems,
    xa_t, ga_t, gga, gx, prod, ext, z, slope, dz, dext, dext_rim, rim_low, rim_high, rim32, halo_bf, halo_f32, low_rows, chunk_rows,
    local_one, local_two, send_sems, recv_sems, halo_send_sems, halo_recv_sems, *part_refs,
):
    blocks, block, per_side = dims
    rows, width = feats.shape
    halo = per_side * block
    ext_rows = rows + 2 * halo
    kernels, _, slots = rules.shape
    groups = kernels // GROUP
    own_chunks, ext_chunks = rows // CHUNK, ext_rows // CHUNK

    def selector(kind, k):
        return one_hot(low_rows[kind, pl.ds(k, 1), :])

    def chunk_of(kind, k):
        return chunk_rows[kind, pl.ds(k, 1), :]

    def own_part(ref):
        return unstack(ref[pl.ds(0, own_chunks * width)], width)

    def rim_part(ref, side):
        size = (halo // CHUNK) * width
        return unstack(ref[pl.ds(own_chunks * width + side * size, size)], width)

    def set_rim(ref, side, value):
        size = (halo // CHUNK) * width
        ref[pl.ds(own_chunks * width + side * size, size)] = stack(value)

    topo = Topology(n_space, n_dp)
    barrier = pltpu.get_barrier_semaphore()
    partners = topo.partners()
    loads = [
        pltpu.make_async_copy(src, dst, load_sems.at[i])
        for i, (src, dst) in enumerate((
            (sends_hbm, sends), (counts_hbm, counts), (rules_hbm, rules), (feats_hbm, feats),
            (cot_hbm, cot), (two_hbm, weight_two), (one_hbm, weight_one),
        ))
    ]
    for load in loads:
        load.start()
    for device in partners:
        pl.semaphore_signal(barrier, inc=1, device_id=device, device_id_type=pl.DeviceIdType.MESH)

    for load in loads[:5]:
        load.wait()
    mask = jnp.concatenate(active_mask(counts, blocks, block, width), axis=1)
    for kind, limit in ((0, ext_rows), (1, rows)):
        index = rules[:, kind, :]
        low_rows[kind] = jnp.where(index < limit, lax.rem(index, CHUNK), -1).astype(F32)
        chunk_rows[kind] = (index // CHUNK).astype(F32)
    xa = feats[...].astype(F32).T * mask
    xa_t[...] = stack(xa.astype(BF16))
    ga_t[...] = stack((cot[...].astype(F32).T * mask).astype(BF16))
    rim_low[0] = pick(sends, 0, per_side, xa, blocks, block).astype(BF16)
    rim_high[0] = pick(sends, 1, per_side, xa, blocks, block).astype(BF16)
    for s in range(2):
        @pl.when(topo.space == 0)
        def _():
            halo_bf[s, 0] = jnp.zeros((width, halo), BF16)
            halo_f32[s, 0] = jnp.zeros((width, halo), F32)

        @pl.when(topo.space == n_space - 1)
        def _():
            halo_bf[s, 1] = jnp.zeros((width, halo), BF16)
            halo_f32[s, 1] = jnp.zeros((width, halo), F32)

    per = width // 16
    pad = local_one.shape[0] - kernels * per
    for local in (local_one, local_two):
        if pad:
            local[pl.ds(kernels * per, pad)] = jnp.zeros((pad, 16, width), F32)
    pl.semaphore_wait(barrier, len(partners))

    def halo_copies(which, to_low, to_high, landing):
        def make(src, side, device):
            return pltpu.make_async_remote_copy(
                src_ref=src,
                dst_ref=landing.at[side],
                send_sem=halo_send_sems.at[which, side],
                recv_sem=halo_recv_sems.at[which, side],
                device_id=(device, topo.dp),
                device_id_type=pl.DeviceIdType.MESH,
            )
        up = make(to_high, 0, lax.rem(topo.space + 1, n_space))
        down = make(to_low, 1, lax.rem(topo.space + n_space - 1, n_space))
        return up, down

    def halo_start(copies):
        up, down = copies

        @pl.when(topo.space < n_space - 1)
        def _():
            up.start()

        @pl.when(topo.space > 0)
        def _():
            down.start()

    def halo_wait(copies):
        up, down = copies

        @pl.when(topo.space < n_space - 1)
        def _():
            up.wait_send()
            down.wait_recv()

        @pl.when(topo.space > 0)
        def _():
            down.wait_send()
            up.wait_recv()

    x_copies = halo_copies(0, rim_low.at[0], rim_high.at[0], halo_bf.at[0])
    halo_start(x_copies)

    loads[5].wait()
    dext[...] = jnp.zeros_like(dext)

    def back_two(i, _):
        weights, placed = [], []
        for j in range(GROUP):
            k = i * GROUP + j
            found = gather(ga_t[...], selector(1, k), chunk_of(1, k), width)
            gga[k] = found
            placed.append(
                dot_nt(spread(found, chunk_of(0, k), ext_chunks), selector(0, k)).astype(BF16)
            )
            weights.append(weight_two[k])
        weights = jnp.concatenate(weights, axis=1)
        for c in range(ext_chunks):
            part = slice(c * width, (c + 1) * width)
            dext[part] += dot(weights, jnp.concatenate([p[part] for p in placed], axis=0))
        return 0

    lax.fori_loop(0, groups, back_two, 0)
    dext_rim[0, 0] = rim_part(dext, 0)
    dext_rim[0, 1] = rim_part(dext, 1)
    dy_copies = halo_copies(1, dext_rim.at[0, 0], dext_rim.at[0, 1], halo_f32.at[0])
    halo_start(dy_copies)

    loads[6].wait()
    halo_wait(x_copies)
    ext[pl.ds(0, own_chunks * width)] = xa_t[...]
    set_rim(ext, 0, halo_bf[0, 0])
    set_rim(ext, 1, halo_bf[0, 1])
    z[...] = jnp.zeros_like(z)

    def forward(i, _):
        weights, placed = [], []
        for j in range(GROUP):
            k = i * GROUP + j
            found = gather(ext[...], selector(0, k), chunk_of(0, k), width)
            gx[k] = found
            placed.append(
                dot_nt(spread(found, chunk_of(1, k), own_chunks), selector(1, k)).astype(BF16)
            )
            weights.append(weight_one[k])
        weights = jnp.concatenate(weights, axis=0)
        for c in range(own_chunks):
            part = slice(c * width, (c + 1) * width)
            z[part] += dot_tn(weights, jnp.concatenate([p[part] for p in placed], axis=0))
        return 0

    lax.fori_loop(0, groups, forward, 0)
    zv = unstack(z[...], width)
    sig = 1.0 / (1.0 + jnp.exp(-zv))
    y = ((zv * sig) * mask).astype(BF16)
    slope[...] = sig * (1.0 + zv * (1.0 - sig)) * mask
    y32 = y.astype(F32)
    rim_low[1] = pick(sends, 0, per_side, y32, blocks, block).astype(BF16)
    rim_high[1] = pick(sends, 1, per_side, y32, blocks, block).astype(BF16)
    y_copies = halo_copies(2, rim_low.at[1], rim_high.at[1], halo_bf.at[1])
    halo_start(y_copies)
    ext[pl.ds(0, own_chunks * width)] = stack(y)

    halo_wait(dy_copies)
    dy = add_back(
        own_part(dext), sends, per_side, halo_f32[0, 0], halo_f32[0, 1], blocks, block
    )
    dz[...] = stack((dy * slope[...]).astype(BF16))

    def grad_first(i, _):
        for j in range(GROUP):
            k = i * GROUP + j
            gathered = gather(dz[...], selector(1, k), chunk_of(1, k), width)
            local_one[pl.ds(k * per, per)] = dot_nt(gx[k], gathered).reshape(per, 16, width)
            prod[k] = dot(weight_one[k], gathered).astype(BF16)
        return 0

    plan, _ = plan_parts(n_space, n_dp, kernels, per)
    depth = len(plan[0][2])
    parts = [None] * 4
    refs = iter(part_refs)
    sem_row = 0
    for side, (local, out) in enumerate(((local_one, out_one), (local_two, out_two))):
        for i, (base, _, axes) in enumerate(plan):
            lands = [next(refs) for _ in range(depth)]
            stages = [next(refs) for _ in range(depth - 1)]
            parts[2 * side + i] = Exchange(
                topo, axes, base, local, out, lands, stages, send_sems.at[sem_row], recv_sems.at[sem_row]
            )
            sem_row += 1
    cut = min(groups, -(-plan[0][1] // (per * GROUP)))

    def go(*which):
        for p in which:
            if parts[p] is not None:
                parts[p].advance()

    def run(start, stop, step):
        if start < stop:
            lax.fori_loop(start, stop, step, 0)

    run(0, cut, grad_first)
    go(0)
    run(cut, groups, grad_first)
    go(1, 0)

    halo_wait(y_copies)
    set_rim(ext, 0, halo_bf[1, 0])
    set_rim(ext, 1, halo_bf[1, 1])

    def grad_second(i, _):
        for j in range(GROUP):
            k = i * GROUP + j
            gathered = gather(ext[...], selector(0, k), chunk_of(0, k), width)
            local_two[pl.ds(k * per, per)] = dot_nt(gathered, gga[k]).reshape(per, 16, width)
        return 0

    run(0, cut, grad_second)
    go(2, 1)
    run(cut, groups, grad_second)
    go(3, 0, 2)
    dext[...] = jnp.zeros_like(dext)

    def back_one(i, _):
        products, selectors = [], []
        for j in range(GROUP):
            k = i * GROUP + j
            products.append(spread(prod[k], chunk_of(0, k), ext_chunks))
            selectors.append(selector(0, k))
        dext[...] += dot_nt(jnp.concatenate(products, axis=1), jnp.concatenate(selectors, axis=1))
        return 0

    cut_a, cut_b = groups // 3, (2 * groups) // 3
    run(0, cut_a, back_one)
    go(1, 3)
    run(cut_a, cut_b, back_one)
    go(0, 2)
    run(cut_b, groups, back_one)
    dext_rim[1, 0] = rim_part(dext, 0)
    dext_rim[1, 1] = rim_part(dext, 1)
    dx_copies = halo_copies(3, dext_rim.at[1, 0], dext_rim.at[1, 1], halo_f32.at[1])
    halo_start(dx_copies)
    go(1, 3, 0, 2, 1, 0)
    halo_wait(dx_copies)
    own = add_back(
        own_part(dext), sends, per_side, halo_f32[1, 0], halo_f32[1, 1], blocks, block
    )
    grad_rows[...] = (own * mask).T
    go(3, 2, 1, 0, 3, 2, 1, 0, 3, 2, 1, 3, 2, 0, 3, 1, 2, 3)
    assert all(p is None or p.level == 2 * depth + 1 for p in parts)


def body(n_space, n_dp, features, cotangent, weight_one, weight_two, rules, halo_send, block_counts):
    feats, cot, links, sends = features[0], cotangent[0], rules[0, 0], halo_send[0, 0]
    rows, width = feats.shape
    blocks = block_counts.shape[1]
    block = rows // blocks
    per_side = sends.shape[1]
    halo = per_side * block
    kernels, slots = links.shape[1:]
    ext_rows = rows + 2 * halo
    per = width // 16
    devices = n_space * n_dp
    plan, tiles = plan_parts(n_space, n_dp, kernels, per)
    sizes = {"core": 2, "side": 2, "rank": n_dp // 2, "line": n_space // 2}
    copies = 2 * sum(n - 1 for n in sizes.values())
    part_scratch = []
    for _ in range(2):
        for _, count, axes in plan:
            lands, stages = part_shapes(sizes, count, axes, width)
            part_scratch += lands + stages
    v, s = pltpu.VMEM, pltpu.SMEM
    grad_rows, one, two = pl.pallas_call(
        functools.partial(whole_kernel, (blocks, block, per_side), n_space, n_dp),
        out_shape=[
            jax.ShapeDtypeStruct((rows, width), F32),
            jax.ShapeDtypeStruct((tiles, 16, width), BF16),
            jax.ShapeDtypeStruct((tiles, 16, width), BF16),
        ],
        in_specs=[pl.BlockSpec(memory_space=pl.ANY)] * 7,
        out_specs=[pl.BlockSpec(memory_space=v)] * 3,
        scratch_shapes=[
            v((rows, width), BF16),
            v((rows, width), BF16),
            v((kernels, width, width), BF16),
            v((kernels, width, width), BF16),
            v((kernels, 2, slots), jnp.int32),
            s((2, per_side), jnp.int32),
            s((1, blocks), jnp.int32),
            pltpu.SemaphoreType.DMA((7,)),
            v((width * rows // CHUNK, CHUNK), BF16),
            v((width * rows // CHUNK, CHUNK), BF16),
            v((kernels, width, slots), BF16),
            v((kernels, width, slots), BF16),
            v((kernels, width, slots), BF16),
            v((width * ext_rows // CHUNK, CHUNK), BF16),
            v((width * rows // CHUNK, CHUNK), F32),
            v((width, rows), F32),
            v((width * rows // CHUNK, CHUNK), BF16),
            v((width * ext_rows // CHUNK, CHUNK), F32),
            v((2, 2, width, halo), F32),
            v((2, width, halo), BF16),
            v((2, width, halo), BF16),
            v((8, 128), F32),
            v((2, 2, width, halo), BF16),
            v((2, 2, width, halo), F32),
            v((2, kernels, slots), F32),
            v((2, kernels, slots), F32),
            v((tiles, 16, width), F32),
            v((tiles, 16, width), F32),
            pltpu.SemaphoreType.DMA((2 * len(plan), copies)),
            pltpu.SemaphoreType.DMA((2 * len(plan), copies)),
            pltpu.SemaphoreType.DMA((4, 2)),
            pltpu.SemaphoreType.DMA((4, 2)),
            *part_scratch,
        ],
        compiler_params=pltpu.CompilerParams(
            collective_id=0, has_side_effects=True, vmem_limit_bytes=VMEM_LIMIT
        ),
    )(feats, cot, weight_one, weight_two, links.transpose(1, 0, 2), sends, block_counts)
    scale = 1.0 / jnp.sqrt(F32(devices * slots))

    def finish(total):
        return total[: kernels * per].astype(F32).reshape(kernels, width, width) * scale

    return (grad_rows[None], finish(one), finish(two))


def solution(mesh):
    n_space, n_dp = mesh.shape["space"], mesh.shape["dp"]
    in_specs = (
        P("dp", "space", None),
        P("dp", "space", None),
        P(),
        P(),
        P("dp", "space", None, None, None),
        P("dp", "space", None, None),
        P("dp", "space"),
    )
    out_specs = (P("dp", "space", None), P(), P())
    return jax.shard_map(
        functools.partial(body, n_space, n_dp), mesh=mesh, in_specs=in_specs, out_specs=out_specs, check_vma=False)
```

```python
import functools

import jax
import jax.numpy as jnp
from jax import lax
from jax.experimental import pallas as pl
from jax.experimental.pallas import tpu as pltpu
from jax.sharding import PartitionSpec as P

F32 = jnp.float32
BF16 = jnp.bfloat16
CHUNK = 256
GROUP = 9
VMEM_LIMIT = 62 * 1024 * 1024


def dot(a, b):
    return jnp.dot(a, b, preferred_element_type=F32)


def dot_nt(a, b):
    return lax.dot_general(a, b, (((1,), (1,)), ((), ())), preferred_element_type=F32)


def dot_tn(a, b):
    return lax.dot_general(a, b, (((0,), (0,)), ((), ())), preferred_element_type=F32)


def one_hot(low_row):
    slots = low_row.shape[1]
    place = lax.broadcasted_iota(jnp.int32, (CHUNK, slots), 0).astype(F32).astype(BF16)
    return jnp.where(
        place == jnp.broadcast_to(low_row.astype(BF16), (CHUNK, slots)),
        jnp.ones((), BF16), jnp.zeros((), BF16),
    )


def gather(table, selector, chunk_row, width):
    found = dot(table, selector)
    chunks = table.shape[0] // width
    chunk = jnp.broadcast_to(chunk_row, (width, chunk_row.shape[1]))
    out = found[:width]
    for c in range(1, chunks):
        out = jnp.where(chunk == c, found[c * width : (c + 1) * width], out)
    return out.astype(BF16)


def spread(values, chunk_row, chunks):
    chunk = jnp.broadcast_to(chunk_row.astype(BF16), values.shape)
    zero = jnp.zeros((), BF16)
    return jnp.concatenate(
        [jnp.where(chunk == jnp.asarray(c, BF16), values, zero) for c in range(chunks)], axis=0
    )


def stack(table):
    return jnp.concatenate(
        [table[:, c : c + CHUNK] for c in range(0, table.shape[1], CHUNK)], axis=0
    )


def unstack(table, width):
    return jnp.concatenate(
        [table[r : r + width] for r in range(0, table.shape[0], width)], axis=1
    )


def active_mask(counts_ref, blocks, block, width):
    lane = lax.broadcasted_iota(jnp.int32, (width, block), 1)
    return [(lane < counts_ref[0, b]).astype(F32) for b in range(blocks)]


def pick(sends_ref, side, per_side, table, blocks, block):
    picked = []
    for j in range(per_side):
        total = 0.0
        for b in range(blocks):
            total = total + jnp.where(
                sends_ref[side, j] == b, table[:, b * block : (b + 1) * block], 0.0
            )
        picked.append(total)
    return jnp.concatenate(picked, axis=1)


def add_back(own, sends_ref, per_side, from_left, from_right, blocks, block):
    out = []
    for b in range(blocks):
        total = own[:, b * block : (b + 1) * block]
        for side, back in ((0, from_left), (1, from_right)):
            for j in range(per_side):
                total = total + jnp.where(
                    sends_ref[side, j] == b, back[:, j * block : (j + 1) * block], 0.0
                )
        out.append(total)
    return jnp.concatenate(out, axis=1)


class Topology:
    def __init__(self, n_space, n_dp):
        self.n_space, self.n_dp = n_space, n_dp
        self.size = {"core": 2, "side": 2, "rank": n_dp // 2, "line": n_space // 2}
        self.space, self.dp = lax.axis_index("space"), lax.axis_index("dp")
        self.at = {
            "core": lax.rem(self.dp, 2), "side": lax.rem(self.space, 2),
            "rank": self.dp // 2, "line": self.space // 2,
        }

    def others(self, axis):
        found = []
        for d in range(1, self.size[axis]):
            index = lax.rem(self.at[axis] + d, self.size[axis])
            at = dict(self.at, **{axis: index})
            found.append((d - 1, index, (at["line"] * 2 + at["side"], at["rank"] * 2 + at["core"])))
        return found

    def partners(self):
        found = [device for axis in self.size for _, _, device in self.others(axis)]
        found += [(lax.rem(self.space + d, self.n_space), self.dp) for d in (1, self.n_space - 1)]
        return found


class Exchange:
    def __init__(self, topo, axes, base, local, out, lands, sends, send_sems, recv_sems):
        self.topo, self.axes, self.local, self.out = topo, axes, local, out
        self.lands, self.sends, self.send_sems, self.recv_sems = lands, sends, send_sems, recv_sems
        self.offset, self.count = base, lands[0].shape[1] * topo.size[axes[0]]
        self.level, self.sem, self.flying, self.stack = 0, 0, [], []

    def copy(self, src, dst, device):
        sem, self.sem = self.sem, self.sem + 1
        made = pltpu.make_async_remote_copy(
            src_ref=src, dst_ref=dst, send_sem=self.send_sems.at[sem], recv_sem=self.recv_sems.at[sem],
            device_id=device, device_id_type=pl.DeviceIdType.MESH,
        )
        made.start()
        self.flying.append(made)

    def advance(self):
        for made in self.flying:
            made.wait()
        self.flying = []
        t, depth = self.topo, len(self.axes)
        if 0 < self.level <= depth:
            axis = self.axes[self.level - 1]
            self.stack.append((self.offset, self.count))
            self.count //= t.size[axis]
            self.offset = self.offset + t.at[axis] * self.count
            own = pl.ds(self.offset, self.count)
            total = self.local[own]
            for slot in range(t.size[axis] - 1):
                total = total + self.lands[self.level - 1][slot].astype(F32)
            if self.level < depth:
                self.local[own] = total
                self.sends[self.level - 1][...] = total.astype(BF16)
            else:
                self.out[own] = total.astype(BF16)
        if self.level < depth:
            axis = self.axes[self.level]
            piece = self.count // t.size[axis]
            for slot, index, device in t.others(axis):
                if self.level == 0:
                    src = self.local.at[pl.ds(self.offset + index * piece, piece)]
                else:
                    src = self.sends[self.level - 1].at[pl.ds(index * piece, piece)]
                self.copy(src, self.lands[self.level].at[slot], device)
        elif self.level < 2 * depth:
            axis = self.axes[2 * depth - 1 - self.level]
            place = self.out.at[pl.ds(self.offset, self.count)]
            for _, _, device in t.others(axis):
                self.copy(place, place, device)
            self.offset, self.count = self.stack.pop()
        self.level += 1


def plan_parts(n_space, n_dp, kernels, per):
    devices = n_space * n_dp
    units = -(-kernels * per // devices)
    first = (units + 1) // 2
    parts = [(0, first * devices, ("core", "side", "rank", "line"))]
    if units > first:
        parts.append((first * devices, (units - first) * devices, ("core", "rank", "side", "line")))
    return parts, units * devices


def part_shapes(sizes, tiles, axes, width):
    lands, sends = [], []
    for level, axis in enumerate(axes):
        if level:
            sends.append(pltpu.VMEM((tiles, 16, width), BF16))
        tiles //= sizes[axis]
        lands.append(pltpu.VMEM((sizes[axis] - 1, tiles, 16, width), BF16 if level else F32))
    return lands, sends


def whole_kernel(
    dims, n_space, n_dp,
    feats_hbm, cot_hbm, one_hbm, two_hbm, rules_hbm, sends_hbm, counts_hbm,
    grad_rows, out_one, out_two,
    feats, cot, weight_one, weight_two, rules, sends, counts, load_sems,
    xa_t, ga_t, gga, gx, prod, ext, z, slope, dz, dext, dext_rim, rim_low, rim_high, rim32, halo_bf, halo_f32, low_rows, chunk_rows,
    local_one, local_two, send_sems, recv_sems, halo_send_sems, halo_recv_sems, *part_refs,
):
    blocks, block, per_side = dims
    rows, width = feats.shape
    halo = per_side * block
    ext_rows = rows + 2 * halo
    kernels, _, slots = rules.shape
    groups = kernels // GROUP
    own_chunks, ext_chunks = rows // CHUNK, ext_rows // CHUNK

    def selector(kind, k):
        return one_hot(low_rows[kind, pl.ds(k, 1), :])

    def chunk_of(kind, k):
        return chunk_rows[kind, pl.ds(k, 1), :]

    def own_part(ref):
        return unstack(ref[pl.ds(0, own_chunks * width)], width)

    def rim_part(ref, side):
        size = (halo // CHUNK) * width
        return unstack(ref[pl.ds(own_chunks * width + side * size, size)], width)

    def set_rim(ref, side, value):
        size = (halo // CHUNK) * width
        ref[pl.ds(own_chunks * width + side * size, size)] = stack(value)

    topo = Topology(n_space, n_dp)
    barrier = pltpu.get_barrier_semaphore()
    partners = topo.partners()
    loads = [
        pltpu.make_async_copy(src, dst, load_sems.at[i])
        for i, (src, dst) in enumerate((
            (sends_hbm, sends), (counts_hbm, counts), (rules_hbm, rules), (feats_hbm, feats),
            (cot_hbm, cot), (two_hbm, weight_two), (one_hbm, weight_one),
        ))
    ]
    for load in loads:
        load.start()
    for device in partners:
        pl.semaphore_signal(barrier, inc=1, device_id=device, device_id_type=pl.DeviceIdType.MESH)

    for load in loads[:5]:
        load.wait()
    mask = jnp.concatenate(active_mask(counts, blocks, block, width), axis=1)
    for kind, limit in ((0, ext_rows), (1, rows)):
        index = rules[:, kind, :]
        low_rows[kind] = jnp.where(index < limit, lax.rem(index, CHUNK), -1).astype(F32)
        chunk_rows[kind] = (index // CHUNK).astype(F32)
    xa = feats[...].astype(F32).T * mask
    xa_t[...] = stack(xa.astype(BF16))
    ga_t[...] = stack((cot[...].astype(F32).T * mask).astype(BF16))
    rim_low[0] = pick(sends, 0, per_side, xa, blocks, block).astype(BF16)
    rim_high[0] = pick(sends, 1, per_side, xa, blocks, block).astype(BF16)
    for s in range(2):
        @pl.when(topo.space == 0)
        def _():
            halo_bf[s, 0] = jnp.zeros((width, halo), BF16)
            halo_f32[s, 0] = jnp.zeros((width, halo), F32)

        @pl.when(topo.space == n_space - 1)
        def _():
            halo_bf[s, 1] = jnp.zeros((width, halo), BF16)
            halo_f32[s, 1] = jnp.zeros((width, halo), F32)

    per = width // 16
    pad = local_one.shape[0] - kernels * per
    for local in (local_one, local_two):
        if pad:
            local[pl.ds(kernels * per, pad)] = jnp.zeros((pad, 16, width), F32)
    pl.semaphore_wait(barrier, len(partners))

    def halo_copies(which, to_low, to_high, landing):
        def make(src, side, device):
            return pltpu.make_async_remote_copy(
                src_ref=src,
                dst_ref=landing.at[side],
                send_sem=halo_send_sems.at[which, side],
                recv_sem=halo_recv_sems.at[which, side],
                device_id=(device, topo.dp),
                device_id_type=pl.DeviceIdType.MESH,
            )
        up = make(to_high, 0, lax.rem(topo.space + 1, n_space))
        down = make(to_low, 1, lax.rem(topo.space + n_space - 1, n_space))
        return up, down

    def halo_start(copies):
        up, down = copies

        @pl.when(topo.space < n_space - 1)
        def _():
            up.start()

        @pl.when(topo.space > 0)
        def _():
            down.start()

    def halo_wait(copies):
        up, down = copies

        @pl.when(topo.space < n_space - 1)
        def _():
            up.wait_send()
            down.wait_recv()

        @pl.when(topo.space > 0)
        def _():
            down.wait_send()
            up.wait_recv()

    x_copies = halo_copies(0, rim_low.at[0], rim_high.at[0], halo_bf.at[0])
    halo_start(x_copies)

    loads[5].wait()
    dext[...] = jnp.zeros_like(dext)

    def members(i):
        return [i * GROUP + j for j in range(GROUP)]

    def back_two(i, _):
        ks = members(i)
        found = [gather(ga_t[...], selector(1, k), chunk_of(1, k), width) for k in ks]
        placed = [
            dot_nt(spread(f, chunk_of(0, k), ext_chunks), selector(0, k)).astype(BF16)
            for f, k in zip(found, ks)
        ]
        weights = jnp.concatenate([weight_two[k] for k in ks], axis=1)
        for c in range(ext_chunks):
            part = slice(c * width, (c + 1) * width)
            dext[part] += dot(weights, jnp.concatenate([p[part] for p in placed], axis=0))
        for f, k in zip(found, ks):
            gga[k] = f
        return 0

    lax.fori_loop(0, groups, back_two, 0)
    dext_rim[0, 0] = rim_part(dext, 0)
    dext_rim[0, 1] = rim_part(dext, 1)
    dy_copies = halo_copies(1, dext_rim.at[0, 0], dext_rim.at[0, 1], halo_f32.at[0])
    halo_start(dy_copies)

    loads[6].wait()
    halo_wait(x_copies)
    ext[pl.ds(0, own_chunks * width)] = xa_t[...]
    set_rim(ext, 0, halo_bf[0, 0])
    set_rim(ext, 1, halo_bf[0, 1])
    z[...] = jnp.zeros_like(z)

    def forward(i, _):
        ks = members(i)
        found = [gather(ext[...], selector(0, k), chunk_of(0, k), width) for k in ks]
        placed = [
            dot_nt(spread(f, chunk_of(1, k), own_chunks), selector(1, k)).astype(BF16)
            for f, k in zip(found, ks)
        ]
        weights = jnp.concatenate([weight_one[k] for k in ks], axis=0)
        for c in range(own_chunks):
            part = slice(c * width, (c + 1) * width)
            z[part] += dot_tn(weights, jnp.concatenate([p[part] for p in placed], axis=0))
        for f, k in zip(found, ks):
            gx[k] = f
        return 0

    lax.fori_loop(0, groups, forward, 0)
    zv = unstack(z[...], width)
    sig = 1.0 / (1.0 + jnp.exp(-zv))
    y = ((zv * sig) * mask).astype(BF16)
    slope[...] = sig * (1.0 + zv * (1.0 - sig)) * mask
    y32 = y.astype(F32)
    rim_low[1] = pick(sends, 0, per_side, y32, blocks, block).astype(BF16)
    rim_high[1] = pick(sends, 1, per_side, y32, blocks, block).astype(BF16)
    y_copies = halo_copies(2, rim_low.at[1], rim_high.at[1], halo_bf.at[1])
    halo_start(y_copies)
    ext[pl.ds(0, own_chunks * width)] = stack(y)

    halo_wait(dy_copies)
    dy = add_back(
        own_part(dext), sends, per_side, halo_f32[0, 0], halo_f32[0, 1], blocks, block
    )
    dz[...] = stack((dy * slope[...]).astype(BF16))

    def grad_first(i, _):
        ks = members(i)
        found = [gather(dz[...], selector(1, k), chunk_of(1, k), width) for k in ks]
        grads = [dot_nt(gx[k], f) for f, k in zip(found, ks)]
        products = [dot(weight_one[k], f).astype(BF16) for f, k in zip(found, ks)]
        for grad, product, k in zip(grads, products, ks):
            local_one[pl.ds(k * per, per)] = grad.reshape(per, 16, width)
            prod[k] = product
        return 0

    plan, _ = plan_parts(n_space, n_dp, kernels, per)
    depth = len(plan[0][2])
    parts = [None] * 4
    refs = iter(part_refs)
    sem_row = 0
    for side, (local, out) in enumerate(((local_one, out_one), (local_two, out_two))):
        for i, (base, _, axes) in enumerate(plan):
            lands = [next(refs) for _ in range(depth)]
            stages = [next(refs) for _ in range(depth - 1)]
            parts[2 * side + i] = Exchange(
                topo, axes, base, local, out, lands, stages, send_sems.at[sem_row], recv_sems.at[sem_row]
            )
            sem_row += 1
    cut = min(groups, -(-plan[0][1] // (per * GROUP)))

    def go(*which):
        for p in which:
            if parts[p] is not None:
                parts[p].advance()

    def run(start, stop, step):
        if start < stop:
            lax.fori_loop(start, stop, step, 0)

    run(0, cut, grad_first)
    go(0)
    run(cut, groups, grad_first)
    go(1, 0)

    halo_wait(y_copies)
    set_rim(ext, 0, halo_bf[1, 0])
    set_rim(ext, 1, halo_bf[1, 1])

    def grad_second(i, _):
        ks = members(i)
        found = [gather(ext[...], selector(0, k), chunk_of(0, k), width) for k in ks]
        grads = [dot_nt(f, gga[k]) for f, k in zip(found, ks)]
        for grad, k in zip(grads, ks):
            local_two[pl.ds(k * per, per)] = grad.reshape(per, 16, width)
        return 0

    run(0, cut, grad_second)
    go(2, 1)
    run(cut, groups, grad_second)
    go(3, 0, 2)
    dext[...] = jnp.zeros_like(dext)

    def back_one(i, _):
        ks = members(i)
        spreads = [spread(prod[k], chunk_of(0, k), ext_chunks) for k in ks]
        selectors = [selector(0, k) for k in ks]
        dext[...] += dot_nt(jnp.concatenate(spreads, axis=1), jnp.concatenate(selectors, axis=1))
        return 0

    cut_a, cut_b = groups // 3, (2 * groups) // 3
    run(0, cut_a, back_one)
    go(1, 3)
    run(cut_a, cut_b, back_one)
    go(0, 2)
    run(cut_b, groups, back_one)
    dext_rim[1, 0] = rim_part(dext, 0)
    dext_rim[1, 1] = rim_part(dext, 1)
    dx_copies = halo_copies(3, dext_rim.at[1, 0], dext_rim.at[1, 1], halo_f32.at[1])
    halo_start(dx_copies)
    go(1, 3, 0, 2, 1, 0)
    halo_wait(dx_copies)
    own = add_back(
        own_part(dext), sends, per_side, halo_f32[1, 0], halo_f32[1, 1], blocks, block
    )
    grad_rows[...] = (own * mask).T
    go(3, 2, 1, 0, 3, 2, 1, 0, 3, 2, 1, 3, 2, 0, 3, 1, 2, 3)
    assert all(p is None or p.level == 2 * depth + 1 for p in parts)


def body(n_space, n_dp, features, cotangent, weight_one, weight_two, rules, halo_send, block_counts):
    feats, cot, links, sends = features[0], cotangent[0], rules[0, 0], halo_send[0, 0]
    rows, width = feats.shape
    blocks = block_counts.shape[1]
    block = rows // blocks
    per_side = sends.shape[1]
    halo = per_side * block
    kernels, slots = links.shape[1:]
    ext_rows = rows + 2 * halo
    per = width // 16
    devices = n_space * n_dp
    plan, tiles = plan_parts(n_space, n_dp, kernels, per)
    sizes = {"core": 2, "side": 2, "rank": n_dp // 2, "line": n_space // 2}
    copies = 2 * sum(n - 1 for n in sizes.values())
    part_scratch = []
    for _ in range(2):
        for _, count, axes in plan:
            lands, stages = part_shapes(sizes, count, axes, width)
            part_scratch += lands + stages
    v, s = pltpu.VMEM, pltpu.SMEM
    grad_rows, one, two = pl.pallas_call(
        functools.partial(whole_kernel, (blocks, block, per_side), n_space, n_dp),
        out_shape=[
            jax.ShapeDtypeStruct((rows, width), F32),
            jax.ShapeDtypeStruct((tiles, 16, width), BF16),
            jax.ShapeDtypeStruct((tiles, 16, width), BF16),
        ],
        in_specs=[pl.BlockSpec(memory_space=pl.ANY)] * 7,
        out_specs=[pl.BlockSpec(memory_space=v)] * 3,
        scratch_shapes=[
            v((rows, width), BF16),
            v((rows, width), BF16),
            v((kernels, width, width), BF16),
            v((kernels, width, width), BF16),
            v((kernels, 2, slots), jnp.int32),
            s((2, per_side), jnp.int32),
            s((1, blocks), jnp.int32),
            pltpu.SemaphoreType.DMA((7,)),
            v((width * rows // CHUNK, CHUNK), BF16),
            v((width * rows // CHUNK, CHUNK), BF16),
            v((kernels, width, slots), BF16),
            v((kernels, width, slots), BF16),
            v((kernels, width, slots), BF16),
            v((width * ext_rows // CHUNK, CHUNK), BF16),
            v((width * rows // CHUNK, CHUNK), F32),
            v((width, rows), F32),
            v((width * rows // CHUNK, CHUNK), BF16),
            v((width * ext_rows // CHUNK, CHUNK), F32),
            v((2, 2, width, halo), F32),
            v((2, width, halo), BF16),
            v((2, width, halo), BF16),
            v((8, 128), F32),
            v((2, 2, width, halo), BF16),
            v((2, 2, width, halo), F32),
            v((2, kernels, slots), F32),
            v((2, kernels, slots), F32),
            v((tiles, 16, width), F32),
            v((tiles, 16, width), F32),
            pltpu.SemaphoreType.DMA((2 * len(plan), copies)),
            pltpu.SemaphoreType.DMA((2 * len(plan), copies)),
            pltpu.SemaphoreType.DMA((4, 2)),
            pltpu.SemaphoreType.DMA((4, 2)),
            *part_scratch,
        ],
        compiler_params=pltpu.CompilerParams(
            collective_id=0, has_side_effects=True, vmem_limit_bytes=VMEM_LIMIT
        ),
    )(feats, cot, weight_one, weight_two, links.transpose(1, 0, 2), sends, block_counts)
    scale = 1.0 / jnp.sqrt(F32(devices * slots))

    def finish(total):
        return total[: kernels * per].astype(F32).reshape(kernels, width, width) * scale

    return (grad_rows[None], finish(one), finish(two))


def solution(mesh):
    n_space, n_dp = mesh.shape["space"], mesh.shape["dp"]
    in_specs = (
        P("dp", "space", None),
        P("dp", "space", None),
        P(),
        P(),
        P("dp", "space", None, None, None),
        P("dp", "space", None, None),
        P("dp", "space"),
    )
    out_specs = (P("dp", "space", None), P(), P())
    return jax.shard_map(
        functools.partial(body, n_space, n_dp), mesh=mesh, in_specs=in_specs, out_specs=out_specs, check_vma=False)
```

```python
import functools

import jax
import jax.numpy as jnp
from jax import lax
from jax.experimental import pallas as pl
from jax.experimental.pallas import tpu as pltpu
from jax.sharding import PartitionSpec as P

F32 = jnp.float32
BF16 = jnp.bfloat16
CHUNK = 256
GROUP = 9
VMEM_LIMIT = 62 * 1024 * 1024


def dot(a, b):
    return jnp.dot(a, b, preferred_element_type=F32)


def dot_nt(a, b):
    return lax.dot_general(a, b, (((1,), (1,)), ((), ())), preferred_element_type=F32)


def dot_tn(a, b):
    return lax.dot_general(a, b, (((0,), (0,)), ((), ())), preferred_element_type=F32)


def one_hot(low_row):
    slots = low_row.shape[1]
    place = lax.broadcasted_iota(jnp.int32, (CHUNK, slots), 0).astype(F32).astype(BF16)
    return jnp.where(
        place == jnp.broadcast_to(low_row.astype(BF16), (CHUNK, slots)),
        jnp.ones((), BF16), jnp.zeros((), BF16),
    )


def gather(table, selector, chunk_row, width):
    found = dot(table, selector)
    chunks = table.shape[0] // width
    chunk = jnp.broadcast_to(chunk_row, (width, chunk_row.shape[1]))
    out = found[:width]
    for c in range(1, chunks):
        out = jnp.where(chunk == c, found[c * width : (c + 1) * width], out)
    return out.astype(BF16)


def spread(values, chunk_row, chunks):
    chunk = jnp.broadcast_to(chunk_row.astype(BF16), values.shape)
    zero = jnp.zeros((), BF16)
    return jnp.concatenate(
        [jnp.where(chunk == jnp.asarray(c, BF16), values, zero) for c in range(chunks)], axis=0
    )


def stack(table):
    return jnp.concatenate(
        [table[:, c : c + CHUNK] for c in range(0, table.shape[1], CHUNK)], axis=0
    )


def unstack(table, width):
    return jnp.concatenate(
        [table[r : r + width] for r in range(0, table.shape[0], width)], axis=1
    )


def active_mask(counts_ref, blocks, block, width):
    lane = lax.broadcasted_iota(jnp.int32, (width, block), 1)
    return [(lane < counts_ref[0, b]).astype(F32) for b in range(blocks)]


def pick(sends_ref, side, per_side, table, blocks, block):
    picked = []
    for j in range(per_side):
        total = 0.0
        for b in range(blocks):
            total = total + jnp.where(
                sends_ref[side, j] == b, table[:, b * block : (b + 1) * block], 0.0
            )
        picked.append(total)
    return jnp.concatenate(picked, axis=1)


def add_back(own, sends_ref, per_side, from_left, from_right, blocks, block):
    out = []
    for b in range(blocks):
        total = own[:, b * block : (b + 1) * block]
        for side, back in ((0, from_left), (1, from_right)):
            for j in range(per_side):
                total = total + jnp.where(
                    sends_ref[side, j] == b, back[:, j * block : (j + 1) * block], 0.0
                )
        out.append(total)
    return jnp.concatenate(out, axis=1)


class Topology:
    def __init__(self, n_space, n_dp):
        self.n_space, self.n_dp = n_space, n_dp
        self.size = {"core": 2, "quad": (n_dp // 2) * 2, "line": n_space // 2}
        self.space, self.dp = lax.axis_index("space"), lax.axis_index("dp")
        self.at = {
            "core": lax.rem(self.dp, 2),
            "quad": (self.dp // 2) * 2 + lax.rem(self.space, 2),
            "line": self.space // 2,
        }

    def others(self, axis):
        found = []
        for d in range(1, self.size[axis]):
            index = lax.rem(self.at[axis] + d, self.size[axis])
            at = dict(self.at, **{axis: index})
            device = (at["line"] * 2 + lax.rem(at["quad"], 2), (at["quad"] // 2) * 2 + at["core"])
            found.append((d - 1, index, device))
        return found

    def partners(self):
        found = [device for axis in self.size for _, _, device in self.others(axis)]
        found += [(lax.rem(self.space + d, self.n_space), self.dp) for d in (1, self.n_space - 1)]
        return found


class Exchange:
    def __init__(self, topo, axes, base, local, out, lands, sends, send_sems, recv_sems):
        self.topo, self.axes, self.local, self.out = topo, axes, local, out
        self.lands, self.sends, self.send_sems, self.recv_sems = lands, sends, send_sems, recv_sems
        self.offset, self.count = base, lands[0].shape[1] * topo.size[axes[0]]
        self.level, self.sem, self.flying, self.stack = 0, 0, [], []

    def copy(self, src, dst, device):
        sem, self.sem = self.sem, self.sem + 1
        made = pltpu.make_async_remote_copy(
            src_ref=src, dst_ref=dst, send_sem=self.send_sems.at[sem], recv_sem=self.recv_sems.at[sem],
            device_id=device, device_id_type=pl.DeviceIdType.MESH,
        )
        made.start()
        self.flying.append(made)

    def advance(self):
        for made in self.flying:
            made.wait()
        self.flying = []
        t, depth = self.topo, len(self.axes)
        if 0 < self.level <= depth:
            axis = self.axes[self.level - 1]
            self.stack.append((self.offset, self.count))
            self.count //= t.size[axis]
            self.offset = self.offset + t.at[axis] * self.count
            own = pl.ds(self.offset, self.count)
            total = self.local[own]
            for slot in range(t.size[axis] - 1):
                total = total + self.lands[self.level - 1][slot].astype(F32)
            if self.level < depth:
                self.local[own] = total
                self.sends[self.level][...] = total.astype(BF16)
            else:
                self.out[own] = total.astype(BF16)
        if self.level < depth:
            axis = self.axes[self.level]
            piece = self.count // t.size[axis]
            for slot, index, device in t.others(axis):
                part = pl.ds(index * piece, piece)
                src = self.sends[self.level].at[part]
                if self.level == 0:
                    src[...] = self.local[pl.ds(self.offset + index * piece, piece)].astype(BF16)
                self.copy(src, self.lands[self.level].at[slot], device)
        elif self.level < 2 * depth:
            axis = self.axes[2 * depth - 1 - self.level]
            place = self.out.at[pl.ds(self.offset, self.count)]
            for _, _, device in t.others(axis):
                self.copy(place, place, device)
            self.offset, self.count = self.stack.pop()
        self.level += 1


def plan_parts(n_space, n_dp, kernels, per):
    devices = n_space * n_dp
    units = -(-kernels * per // devices)
    first = (units + 1) // 2
    parts = [(0, first * devices, ("core", "quad", "line"))]
    if units > first:
        parts.append((first * devices, (units - first) * devices, ("core", "quad", "line")))
    return parts, units * devices


def part_shapes(sizes, tiles, axes, width):
    lands, sends = [], []
    for level, axis in enumerate(axes):
        sends.append(pltpu.VMEM((tiles, 16, width), BF16))
        tiles //= sizes[axis]
        lands.append(pltpu.VMEM((sizes[axis] - 1, tiles, 16, width), BF16))
    return lands, sends


def whole_kernel(
    dims, n_space, n_dp,
    feats_hbm, cot_hbm, one_hbm, two_hbm, rules_hbm, sends_hbm, counts_hbm,
    grad_rows, out_one, out_two,
    feats, cot, weight_one, weight_two, rules, sends, counts, load_sems,
    xa_t, ga_t, gga, gx, prod, ext, z, slope, dz, dext, dext_rim, rim_low, rim_high, rim32, halo_bf, halo_f32, low_rows, chunk_rows,
    local_one, local_two, send_sems, recv_sems, halo_send_sems, halo_recv_sems, *part_refs,
):
    blocks, block, per_side = dims
    rows, width = feats.shape
    halo = per_side * block
    ext_rows = rows + 2 * halo
    kernels, _, slots = rules.shape
    groups = kernels // GROUP
    own_chunks, ext_chunks = rows // CHUNK, ext_rows // CHUNK

    def selector(kind, k):
        return one_hot(low_rows[kind, pl.ds(k, 1), :])

    def chunk_of(kind, k):
        return chunk_rows[kind, pl.ds(k, 1), :]

    def own_part(ref):
        return unstack(ref[pl.ds(0, own_chunks * width)], width)

    def rim_part(ref, side):
        size = (halo // CHUNK) * width
        return unstack(ref[pl.ds(own_chunks * width + side * size, size)], width)

    def set_rim(ref, side, value):
        size = (halo // CHUNK) * width
        ref[pl.ds(own_chunks * width + side * size, size)] = stack(value)

    topo = Topology(n_space, n_dp)
    barrier = pltpu.get_barrier_semaphore()
    partners = topo.partners()
    loads = [
        pltpu.make_async_copy(src, dst, load_sems.at[i])
        for i, (src, dst) in enumerate((
            (sends_hbm, sends), (counts_hbm, counts), (rules_hbm, rules), (feats_hbm, feats),
            (cot_hbm, cot), (two_hbm, weight_two), (one_hbm, weight_one),
        ))
    ]
    for load in loads:
        load.start()
    for device in partners:
        pl.semaphore_signal(barrier, inc=1, device_id=device, device_id_type=pl.DeviceIdType.MESH)

    for load in loads[:5]:
        load.wait()
    mask = jnp.concatenate(active_mask(counts, blocks, block, width), axis=1)
    for kind, limit in ((0, ext_rows), (1, rows)):
        index = rules[:, kind, :]
        low_rows[kind] = jnp.where(index < limit, lax.rem(index, CHUNK), -1).astype(F32)
        chunk_rows[kind] = (index // CHUNK).astype(F32)
    xa = feats[...].astype(F32).T * mask
    xa_t[...] = stack(xa.astype(BF16))
    ga_t[...] = stack((cot[...].astype(F32).T * mask).astype(BF16))
    rim_low[0] = pick(sends, 0, per_side, xa, blocks, block).astype(BF16)
    rim_high[0] = pick(sends, 1, per_side, xa, blocks, block).astype(BF16)
    for s in range(2):
        @pl.when(topo.space == 0)
        def _():
            halo_bf[s, 0] = jnp.zeros((width, halo), BF16)
            halo_f32[s, 0] = jnp.zeros((width, halo), F32)

        @pl.when(topo.space == n_space - 1)
        def _():
            halo_bf[s, 1] = jnp.zeros((width, halo), BF16)
            halo_f32[s, 1] = jnp.zeros((width, halo), F32)

    per = width // 16
    pad = local_one.shape[0] - kernels * per
    for local in (local_one, local_two):
        if pad:
            local[pl.ds(kernels * per, pad)] = jnp.zeros((pad, 16, width), F32)
    pl.semaphore_wait(barrier, len(partners))

    def halo_copies(which, to_low, to_high, landing):
        def make(src, side, device):
            return pltpu.make_async_remote_copy(
                src_ref=src,
                dst_ref=landing.at[side],
                send_sem=halo_send_sems.at[which, side],
                recv_sem=halo_recv_sems.at[which, side],
                device_id=(device, topo.dp),
                device_id_type=pl.DeviceIdType.MESH,
            )
        up = make(to_high, 0, lax.rem(topo.space + 1, n_space))
        down = make(to_low, 1, lax.rem(topo.space + n_space - 1, n_space))
        return up, down

    def halo_start(copies):
        up, down = copies

        @pl.when(topo.space < n_space - 1)
        def _():
            up.start()

        @pl.when(topo.space > 0)
        def _():
            down.start()

    def halo_wait(copies):
        up, down = copies

        @pl.when(topo.space < n_space - 1)
        def _():
            up.wait_send()
            down.wait_recv()

        @pl.when(topo.space > 0)
        def _():
            down.wait_send()
            up.wait_recv()

    x_copies = halo_copies(0, rim_low.at[0], rim_high.at[0], halo_bf.at[0])
    halo_start(x_copies)

    loads[5].wait()
    dext[...] = jnp.zeros_like(dext)

    def members(i):
        return [i * GROUP + j for j in range(GROUP)]

    def back_two(i, _):
        ks = members(i)
        found = [gather(ga_t[...], selector(1, k), chunk_of(1, k), width) for k in ks]
        placed = [
            dot_nt(spread(f, chunk_of(0, k), ext_chunks), selector(0, k)).astype(BF16)
            for f, k in zip(found, ks)
        ]
        weights = jnp.concatenate([weight_two[k] for k in ks], axis=1)
        for c in range(ext_chunks):
            part = slice(c * width, (c + 1) * width)
            dext[part] += dot(weights, jnp.concatenate([p[part] for p in placed], axis=0))
        for f, k in zip(found, ks):
            gga[k] = f
        return 0

    lax.fori_loop(0, groups, back_two, 0)
    dext_rim[0, 0] = rim_part(dext, 0)
    dext_rim[0, 1] = rim_part(dext, 1)
    dy_copies = halo_copies(1, dext_rim.at[0, 0], dext_rim.at[0, 1], halo_f32.at[0])
    halo_start(dy_copies)

    loads[6].wait()
    halo_wait(x_copies)
    ext[pl.ds(0, own_chunks * width)] = xa_t[...]
    set_rim(ext, 0, halo_bf[0, 0])
    set_rim(ext, 1, halo_bf[0, 1])
    z[...] = jnp.zeros_like(z)

    def forward(i, _):
        ks = members(i)
        found = [gather(ext[...], selector(0, k), chunk_of(0, k), width) for k in ks]
        placed = [
            dot_nt(spread(f, chunk_of(1, k), own_chunks), selector(1, k)).astype(BF16)
            for f, k in zip(found, ks)
        ]
        weights = jnp.concatenate([weight_one[k] for k in ks], axis=0)
        for c in range(own_chunks):
            part = slice(c * width, (c + 1) * width)
            z[part] += dot_tn(weights, jnp.concatenate([p[part] for p in placed], axis=0))
        for f, k in zip(found, ks):
            gx[k] = f
        return 0

    lax.fori_loop(0, groups, forward, 0)
    zv = unstack(z[...], width)
    sig = 1.0 / (1.0 + jnp.exp(-zv))
    y = ((zv * sig) * mask).astype(BF16)
    slope[...] = sig * (1.0 + zv * (1.0 - sig)) * mask
    y32 = y.astype(F32)
    rim_low[1] = pick(sends, 0, per_side, y32, blocks, block).astype(BF16)
    rim_high[1] = pick(sends, 1, per_side, y32, blocks, block).astype(BF16)
    y_copies = halo_copies(2, rim_low.at[1], rim_high.at[1], halo_bf.at[1])
    halo_start(y_copies)
    ext[pl.ds(0, own_chunks * width)] = stack(y)

    halo_wait(dy_copies)
    dy = add_back(
        own_part(dext), sends, per_side, halo_f32[0, 0], halo_f32[0, 1], blocks, block
    )
    dz[...] = stack((dy * slope[...]).astype(BF16))

    def grad_first(i, _):
        ks = members(i)
        found = [gather(dz[...], selector(1, k), chunk_of(1, k), width) for k in ks]
        grads = [dot_nt(gx[k], f) for f, k in zip(found, ks)]
        products = [dot(weight_one[k], f).astype(BF16) for f, k in zip(found, ks)]
        for grad, product, k in zip(grads, products, ks):
            local_one[pl.ds(k * per, per)] = grad.reshape(per, 16, width)
            prod[k] = product
        return 0

    plan, _ = plan_parts(n_space, n_dp, kernels, per)
    depth = len(plan[0][2])
    parts = [None] * 4
    refs = iter(part_refs)
    sem_row = 0
    for side, (local, out) in enumerate(((local_one, out_one), (local_two, out_two))):
        for i, (base, _, axes) in enumerate(plan):
            lands = [next(refs) for _ in range(depth)]
            stages = [next(refs) for _ in range(depth)]
            parts[2 * side + i] = Exchange(
                topo, axes, base, local, out, lands, stages, send_sems.at[sem_row], recv_sems.at[sem_row]
            )
            sem_row += 1
    cut = min(groups, -(-plan[0][1] // (per * GROUP)))

    def go(*which):
        for p in which:
            if parts[p] is not None:
                parts[p].advance()

    def run(start, stop, step):
        if start < stop:
            lax.fori_loop(start, stop, step, 0)

    run(0, cut, grad_first)
    go(0)
    run(cut, groups, grad_first)
    go(1, 0)

    halo_wait(y_copies)
    set_rim(ext, 0, halo_bf[1, 0])
    set_rim(ext, 1, halo_bf[1, 1])

    def grad_second(i, _):
        ks = members(i)
        found = [gather(ext[...], selector(0, k), chunk_of(0, k), width) for k in ks]
        grads = [dot_nt(f, gga[k]) for f, k in zip(found, ks)]
        for grad, k in zip(grads, ks):
            local_two[pl.ds(k * per, per)] = grad.reshape(per, 16, width)
        return 0

    run(0, cut, grad_second)
    go(2, 1)
    run(cut, groups, grad_second)
    go(3, 0, 2)
    dext[...] = jnp.zeros_like(dext)

    def back_one(i, _):
        ks = members(i)
        spreads = [spread(prod[k], chunk_of(0, k), ext_chunks) for k in ks]
        selectors = [selector(0, k) for k in ks]
        dext[...] += dot_nt(jnp.concatenate(spreads, axis=1), jnp.concatenate(selectors, axis=1))
        return 0

    cut_a, cut_b = groups // 3, (2 * groups) // 3
    run(0, cut_a, back_one)
    go(1, 3)
    run(cut_a, cut_b, back_one)
    go(0, 2)
    run(cut_b, groups, back_one)
    dext_rim[1, 0] = rim_part(dext, 0)
    dext_rim[1, 1] = rim_part(dext, 1)
    dx_copies = halo_copies(3, dext_rim.at[1, 0], dext_rim.at[1, 1], halo_f32.at[1])
    halo_start(dx_copies)
    go(1, 3, 0, 2, 1, 0)
    halo_wait(dx_copies)
    own = add_back(
        own_part(dext), sends, per_side, halo_f32[1, 0], halo_f32[1, 1], blocks, block
    )
    grad_rows[...] = (own * mask).T
    go(3, 2, 1, 0, 3, 2, 1, 3, 2, 3)
    assert all(p is None or p.level == 2 * depth + 1 for p in parts)


def body(n_space, n_dp, features, cotangent, weight_one, weight_two, rules, halo_send, block_counts):
    feats, cot, links, sends = features[0], cotangent[0], rules[0, 0], halo_send[0, 0]
    rows, width = feats.shape
    blocks = block_counts.shape[1]
    block = rows // blocks
    per_side = sends.shape[1]
    halo = per_side * block
    kernels, slots = links.shape[1:]
    ext_rows = rows + 2 * halo
    per = width // 16
    devices = n_space * n_dp
    plan, tiles = plan_parts(n_space, n_dp, kernels, per)
    sizes = {"core": 2, "quad": (n_dp // 2) * 2, "line": n_space // 2}
    copies = 2 * sum(n - 1 for n in sizes.values())
    part_scratch = []
    for _ in range(2):
        for _, count, axes in plan:
            lands, stages = part_shapes(sizes, count, axes, width)
            part_scratch += lands + stages
    v, s = pltpu.VMEM, pltpu.SMEM
    grad_rows, one, two = pl.pallas_call(
        functools.partial(whole_kernel, (blocks, block, per_side), n_space, n_dp),
        out_shape=[
            jax.ShapeDtypeStruct((rows, width), F32),
            jax.ShapeDtypeStruct((tiles, 16, width), BF16),
            jax.ShapeDtypeStruct((tiles, 16, width), BF16),
        ],
        in_specs=[pl.BlockSpec(memory_space=pl.ANY)] * 7,
        out_specs=[pl.BlockSpec(memory_space=v)] * 3,
        scratch_shapes=[
            v((rows, width), BF16),
            v((rows, width), BF16),
            v((kernels, width, width), BF16),
            v((kernels, width, width), BF16),
            v((kernels, 2, slots), jnp.int32),
            s((2, per_side), jnp.int32),
            s((1, blocks), jnp.int32),
            pltpu.SemaphoreType.DMA((7,)),
            v((width * rows // CHUNK, CHUNK), BF16),
            v((width * rows // CHUNK, CHUNK), BF16),
            v((kernels, width, slots), BF16),
            v((kernels, width, slots), BF16),
            v((kernels, width, slots), BF16),
            v((width * ext_rows // CHUNK, CHUNK), BF16),
            v((width * rows // CHUNK, CHUNK), F32),
            v((width, rows), F32),
            v((width * rows // CHUNK, CHUNK), BF16),
            v((width * ext_rows // CHUNK, CHUNK), F32),
            v((2, 2, width, halo), F32),
            v((2, width, halo), BF16),
            v((2, width, halo), BF16),
            v((8, 128), F32),
            v((2, 2, width, halo), BF16),
            v((2, 2, width, halo), F32),
            v((2, kernels, slots), F32),
            v((2, kernels, slots), F32),
            v((tiles, 16, width), F32),
            v((tiles, 16, width), F32),
            pltpu.SemaphoreType.DMA((2 * len(plan), copies)),
            pltpu.SemaphoreType.DMA((2 * len(plan), copies)),
            pltpu.SemaphoreType.DMA((4, 2)),
            pltpu.SemaphoreType.DMA((4, 2)),
            *part_scratch,
        ],
        compiler_params=pltpu.CompilerParams(
            collective_id=0, has_side_effects=True, vmem_limit_bytes=VMEM_LIMIT
        ),
    )(feats, cot, weight_one, weight_two, links.transpose(1, 0, 2), sends, block_counts)
    scale = 1.0 / jnp.sqrt(F32(devices * slots))

    def finish(total):
        return total[: kernels * per].astype(F32).reshape(kernels, width, width) * scale

    return (grad_rows[None], finish(one), finish(two))


def solution(mesh):
    n_space, n_dp = mesh.shape["space"], mesh.shape["dp"]
    in_specs = (
        P("dp", "space", None),
        P("dp", "space", None),
        P(),
        P(),
        P("dp", "space", None, None, None),
        P("dp", "space", None, None),
        P("dp", "space"),
    )
    out_specs = (P("dp", "space", None), P(), P())
    return jax.shard_map(
        functools.partial(body, n_space, n_dp), mesh=mesh, in_specs=in_specs, out_specs=out_specs, check_vma=False)
```
